256 devices in a mesh: dp: 32 (over x_hi, z, core), fsdp: 8 (over x_lo, y).
Axes of the slice: x: 4 (x_hi: 2, x_lo: 2; x = x_hi * 2 + x_lo), y: 4, z: 8, core: 2. Of those that a mesh axis runs over, the one named last changes fastest.
Arguments:
- states: bfloat16 [49152, 5120], P(('dp', 'fsdp')), may hold values from -24 to 24
- steps: int32 [256], P(('dp', 'fsdp')), may hold values from 0 to 999
- frozen_query_rows: bfloat16 [49152, 5120], P(('dp', 'fsdp')), may hold values from -6 to 6
- frozen_key_rows: bfloat16 [49152, 5120], P(('dp', 'fsdp')), may hold values from -18 to 18
- frozen_value_rows: bfloat16 [49152, 5120], P(('dp', 'fsdp')), may hold values from -6 to 6
- cotangent: bfloat16 [49152, 5120], P(('dp', 'fsdp')), may hold values from -24 to 24
- adapter_down_maps: bfloat16 [2, 5120, 128], P(None, 'fsdp'), may hold values from -0.078125 to 0.078125
- adapter_up_maps: bfloat16 [2, 128, 5120], P(None, None, 'fsdp'), may hold values from -0.5 to 0.5
Outputs:
- grad_down: float32 [2, 5120, 128], P(None, 'fsdp')
- grad_up: float32 [2, 128, 5120], P(None, None, 'fsdp')
The draws below stay inside these ranges and needn't reach their ends.
All inputs are finite; a program needn't handle non-finite values.
Results may differ from the reference program's by a relative error of at most 0.012.
Values may be sent and summed in bfloat16 or wider, within the bound.
No kernel may reach another device: no remote copies, remote signals or barrier semaphores. Data moves between devices by JAX's collectives and lax.ppermute only.
A program may use at most 128 MiB of HBM per device.

```python
import math
import jax
import jax.numpy as jnp
from jax import lax

MODEL_WIDTH = 5120
HEADS = 40
ADAPTER_RANK = 128
CLIP_LEN = 192
NSTEPS = 1000
CLIPS = 256
TOKENS = 49152


def draw_frozen_query_rows(key, part):
    drawn_key = jax.random.fold_in(key, 5)
    values = jnp.clip(jax.random.normal(drawn_key, (TOKENS, MODEL_WIDTH), jnp.float32), -6.0, 6.0)
    return values.astype(jnp.bfloat16)


def draw_frozen_key_rows(key, part):
    drawn_key = jax.random.fold_in(key, 7)
    base_key = jax.random.fold_in(drawn_key, 0)
    values = jnp.clip(jax.random.normal(base_key, (TOKENS, MODEL_WIDTH), jnp.float32), -6.0, 6.0)
    return values.astype(jnp.bfloat16)


def with_ends(array, stream_key, low, largest):
    place = [jax.random.randint(jax.random.fold_in(stream_key, axis), (), 0, length) for axis, length in enumerate(array.shape)]
    widest = array.shape.index(max(array.shape))
    next_to = place[:widest] + [(place[widest] + 1) % array.shape[widest]] + place[widest + 1:]
    return array.at[tuple(place)].set(low).at[tuple(next_to)].set(largest)


def strengthened(values, stream_key, source, target, parts, factor):
    owner, partner = [(jnp.arange(values.shape[axis_at]) // (values.shape[axis_at] // parts)).reshape([-1 if axis == axis_at else 1 for axis in range(values.ndim)]) for axis_at in (source, target)]
    chosen = jax.random.permutation(stream_key, parts)[partner]
    strong = (owner == chosen) | (owner == (partner + parts // 2) % parts)
    return jnp.where(strong, factor * values, values)


def block_levels(key, dims, shards, smallest, high):
    loudness, own = 1.0, jax.random.fold_in(key, 6)
    for dim, blocks in shards:
        draws = jnp.exp(jax.random.uniform(jax.random.fold_in(own, dim), (blocks,), jnp.float32, smallest / len(shards), high / len(shards)))
        loudness = loudness * jnp.repeat(draws, dims[dim] // blocks).reshape([-1 if axis == dim else 1 for axis in range(len(dims))])
    return loudness


def bell_draw(stream_key, shape, scale, limit, shards=(), held_as=jnp.bfloat16):
    drawn = scale * jax.random.normal(stream_key, shape, jnp.float32)
    if shards:
        drawn = drawn * block_levels(stream_key, shape, shards, -0.22, 0.18)
    return jnp.clip(drawn, -limit, limit).astype(held_as)


def heavy_noise(rng, shape, scale, limit, cuts, heavy, dtype=jnp.bfloat16):
    drawn = scale * jax.random.normal(rng, shape, jnp.float32)
    if cuts:
        drawn = drawn * block_levels(rng, shape, cuts, -0.22, 0.18)
    return jnp.clip(strengthened(drawn, jax.random.fold_in(rng, 3), *heavy), -limit, limit).astype(dtype)


def setup_inputs(seed: int = 0) -> dict:
    key_list = jax.random.split(jax.random.key(seed), 9)
    states = heavy_noise(key_list[0], (TOKENS, MODEL_WIDTH), 1.0, 24.0, ((0, 256),), (0, 1, 256, 6.0))
    steps = with_ends(jax.random.randint(key_list[1], (CLIPS,), 0, NSTEPS), jax.random.fold_in(key_list[1], 1), 0, NSTEPS - 1).astype(jnp.int32)
    frozen_query_rows = draw_frozen_query_rows(jax.random.fold_in(key_list[8], 71), 0)
    frozen_key_rows = draw_frozen_key_rows(jax.random.fold_in(key_list[8], 71), 0)
    frozen_value_rows = bell_draw(key_list[4], (TOKENS, MODEL_WIDTH), 1.0, 6.0, ((0, 256),))
    cotangent = heavy_noise(key_list[5], (TOKENS, MODEL_WIDTH), 1.0, 24.0, ((0, 256),), (0, 1, 256, 6.0))
    adapter_down_maps = bell_draw(key_list[6], (2, MODEL_WIDTH, ADAPTER_RANK), MODEL_WIDTH ** -0.5, 0.078125, ((1, 8),))
    adapter_up_maps = bell_draw(key_list[7], (2, ADAPTER_RANK, MODEL_WIDTH), ADAPTER_RANK ** -0.5, 0.5, ((2, 8),))
    return dict(states=states, steps=steps, frozen_query_rows=frozen_query_rows, frozen_key_rows=frozen_key_rows, frozen_value_rows=frozen_value_rows, cotangent=cotangent, adapter_down_maps=adapter_down_maps, adapter_up_maps=adapter_up_maps)


def rounded(value):
    return lax.optimization_barrier(value.astype(jnp.bfloat16)).astype(jnp.float32)

def clip_objective(down_matrix, up_matrix, states, frozen_query_rows, frozen_key_rows, frozen_value_rows, cotangent, weight):
    highest = lax.Precision.HIGHEST
    length = states.shape[0]
    width = states.shape[1]
    head_size = width // HEADS
    inputs = states.astype(jnp.float32)
    center = inputs - lax.optimization_barrier(jnp.mean(inputs, axis=1, keepdims=True))
    spread = lax.optimization_barrier(jnp.mean(center * center, axis=1, keepdims=True))
    normed = rounded(center * lax.rsqrt(spread + 1e-06))
    low = rounded(jnp.einsum('td,jdr->jtr', normed, down_matrix, precision=highest))
    delta = jnp.einsum('jtr,jrd->jtd', low, up_matrix, precision=highest)
    query = rounded(frozen_query_rows.astype(jnp.float32) + delta[0]).reshape(length, HEADS, head_size)
    value = rounded(frozen_value_rows.astype(jnp.float32) + delta[1]).reshape(length, HEADS, head_size)
    keys = frozen_key_rows.astype(jnp.float32).reshape(length, HEADS, head_size)
    scores = jnp.einsum('qhe,khe->hqk', query, keys, precision=highest) * (1.0 / math.sqrt(head_size))
    probs = rounded(jax.nn.softmax(scores, axis=-1))
    attended = jnp.einsum('hqk,khe->qhe', probs, value, precision=highest).reshape(length, width)
    return weight * jnp.sum(attended * cotangent.astype(jnp.float32))

def reference(states, steps, frozen_query_rows, frozen_key_rows, frozen_value_rows, cotangent, adapter_down_maps, adapter_up_maps):
    down_matrix = adapter_down_maps.astype(jnp.float32)
    up_matrix = adapter_up_maps.astype(jnp.float32)
    weights = (steps.astype(jnp.float32) + 1.0) / NSTEPS
    shaped = [a.reshape(CLIPS, CLIP_LEN, MODEL_WIDTH) for a in (states, frozen_query_rows, frozen_key_rows, frozen_value_rows, cotangent)]
    gradient_fn = jax.grad(clip_objective, argnums=(0, 1))

    def accumulate(carry, item):
        grads = gradient_fn(down_matrix, up_matrix, item[0], item[1], item[2], item[3], item[4], item[5])
        return ((carry[0] + grads[0], carry[1] + grads[1]), None)
    start = (jnp.zeros(down_matrix.shape, jnp.float32), jnp.zeros(up_matrix.shape, jnp.float32))
    totals, _ = lax.scan(accumulate, start, (shaped[0], shaped[1], shaped[2], shaped[3], shaped[4], weights))
    factor = 1.0 / math.sqrt(TOKENS)
    return (totals[0] * factor, totals[1] * factor)
```

```python
import functools
import math

import jax
import jax.numpy as jnp
from jax import lax
from jax.experimental import pallas as pl
from jax.experimental.pallas import tpu as pltpu
from jax.sharding import PartitionSpec as P

HEADS = 40
NSTEPS = 1000
AXES = ("dp", "fsdp")
NX, NY, NZ, NC = 4, 4, 8, 2
BF16 = jnp.bfloat16
F32 = jnp.float32

CLIP = 192
WIDTH = 5120
HALF = WIDTH // 2
SHARD = 640
RANK = 128
HEAD = 128
LOCAL_HEADS = SHARD // HEAD
NORM_ROWS = 32
VMEM_LIMIT = 24 * 1024 * 1024


def linear(x, y, z, c):
    x, y, z, c = x % NX, y % NY, z % NZ, c % NC
    return (((x // 2) * NZ + z) * NC + c) * 8 + (x % 2) * NY + y


def permutation(target):
    pairs = []
    for x in range(NX):
        for y in range(NY):
            for z in range(NZ):
                for c in range(NC):
                    pairs.append((linear(x, y, z, c), linear(*target(x, y, z, c))))
    return pairs


def send(value, target):
    return lax.ppermute(value, AXES, permutation(target))


def swap_cores(value):
    return send(value, lambda x, y, z, c: (x, y, z, 1 - c))


def send_y(value, step):
    return send(value, lambda x, y, z, c: (x, y + step, z, c))


Z_GROUPS = [
    [linear(x, y, z, c) for z in range(NZ)]
    for x in range(NX)
    for y in range(NY)
    for c in range(NC)
]


def exchange_z(value):
    return lax.all_to_all(value, AXES, 0, 0, axis_index_groups=Z_GROUPS, tiled=True)


def dot(a, b, ca, cb):
    return lax.dot_general(a, b, (((ca,), (cb,)), ((), ())), preferred_element_type=F32)


def whole(shape):
    return pl.BlockSpec(shape, lambda *_: (0,) * len(shape))


def normalize_kernel(place, states, q, k, v, g, nown, nsend):
    mine = pl.multiple_of(place[0] * HALF, HALF)
    other = pl.multiple_of((1 - place[0]) * HALF, HALF)
    for start in range(0, NORM_ROWS, 16):
        rows = slice(start, start + 16)
        inputs = states[rows, :].astype(F32)
        center = inputs - jnp.mean(inputs, axis=1, keepdims=True)
        spread = jnp.mean(center * center, axis=1, keepdims=True)
        inverse = lax.rsqrt(spread + 1e-06)
        mean = jnp.mean(inputs, axis=1, keepdims=True)
        for begin, out in ((mine, nown), (other, nsend.at[4])):
            part = states[rows, pl.ds(begin, HALF)].astype(F32)
            out[rows, :] = ((part - mean) * inverse).astype(BF16)
    for n, src in enumerate((q, k, v, g)):
        nsend[n] = src[...]


def normalize(place, states, q, k, v, g):
    half = pl.BlockSpec((NORM_ROWS, HALF), lambda i, place: (i, 1 - place[0]))
    return pl.pallas_call(
        normalize_kernel,
        grid_spec=pltpu.PrefetchScalarGridSpec(
            num_scalar_prefetch=1,
            grid=(CLIP // NORM_ROWS,),
            in_specs=[pl.BlockSpec((NORM_ROWS, WIDTH), lambda i, place: (i, 0))] + [half] * 4,
            out_specs=(
                pl.BlockSpec((NORM_ROWS, HALF), lambda i, place: (i, 0)),
                pl.BlockSpec((5, NORM_ROWS, HALF), lambda i, place: (0, i, 0)),
            ),
        ),
        out_shape=(
            jax.ShapeDtypeStruct((CLIP, HALF), BF16),
            jax.ShapeDtypeStruct((5, CLIP, HALF), BF16),
        ),
        compiler_params=pltpu.CompilerParams(vmem_limit_bytes=VMEM_LIMIT),
        cost_estimate=pl.CostEstimate(flops=0, bytes_accessed=14000000, transcendentals=0),
        name="normalize",
    )(place, states, q, k, v, g)


def lower_kernel(place, nown, npeer, own0, other0, own, other, weight, out):
    core, y = place[2], place[1]
    for clip in range(2):
        totals = [jnp.zeros((CLIP, RANK), F32) for _ in range(2)]
        for step in range(NY):
            start = pl.multiple_of(lax.rem(y + step, NY) * SHARD, SHARD)
            if clip == 0:
                rows = nown[:, pl.ds(start, SHARD)]
            else:
                rows = npeer[0, :, pl.ds(start, SHARD)]
            totals[0] += dot(rows, own[step - 1] if step else own0[0], 1, 0)
            totals[1] += dot(rows, other[step - 1] if step else other0[0], 1, 0)
        out[clip, core, :CLIP] = totals[0]
        out[clip, 1 - core, :CLIP] = totals[1]
        out[clip, 0, CLIP:] = weight[...]
        out[clip, 1, CLIP:] = weight[...]


def lower(place, nown, peer, *downs_and_weight):
    return pl.pallas_call(
        lower_kernel,
        grid=(1,),
        out_shape=jax.ShapeDtypeStruct((2, 2, CLIP + 8, RANK), F32),
        in_specs=[
            pl.BlockSpec(memory_space=pltpu.SMEM),
            whole((CLIP, HALF)),
            pl.BlockSpec((1, CLIP, HALF), lambda i: (4, 0, 0)),
        ]
        + [whole(a.shape) for a in downs_and_weight],
        out_specs=whole((2, 2, CLIP + 8, RANK)),
        compiler_params=pltpu.CompilerParams(vmem_limit_bytes=VMEM_LIMIT),
        name="lower",
    )(place, nown, peer, *downs_and_weight)


def attend_kernel(step, place, *refs):
    q0, k0, v0, g0, q1, k1, v1, g1, up_own, up_other = refs[:10]
    if step == 0:
        low_mine, low_peer, gup, dlow, low, weights, ups, dqs, dvs = refs[10:]
        for j in range(2):
            for clip in range(2):
                total = low_mine[clip, j, :CLIP] + low_peer[1 - clip, j, :CLIP]
                low[j, clip * CLIP : (clip + 1) * CLIP] = total.astype(BF16)
        weights[0] = low_mine[0, 0, CLIP:]
        weights[1] = low_peer[0, 0, CLIP:]
    else:
        low, weights, dlow_in, gup, dlow, ups, dqs, dvs = refs[10:]
    core = place[2]
    scale = 1.0 / math.sqrt(HEAD)
    slot = 0 if up_own.shape[0] == 1 else step - 1
    ups[core] = up_own[slot]
    ups[1 - core] = up_other[slot]
    for clip in range(2):
        rows = slice(clip * CLIP, (clip + 1) * CLIP)
        weight = weights[clip, :1]
        if clip == 0:
            q, k, v, g = (r[...] for r in (q0, k0, v0, g0))
        else:
            q, k, v, g = (r[0] for r in (q1, k1, v1, g1))
        query = (q.astype(F32) + dot(low[0, rows], ups[0], 1, 0)).astype(BF16)
        value = (v.astype(F32) + dot(low[1, rows], ups[1], 1, 0)).astype(BF16)
        for h in range(LOCAL_HEADS):
            cols = slice(h * HEAD, (h + 1) * HEAD)
            kh, gh = k[:, cols], g[:, cols]
            scores = dot(kh, query[:, cols], 1, 1) * scale
            powers = jnp.exp(scores - jnp.max(scores, axis=0, keepdims=True))
            probs = powers * (1.0 / jnp.sum(powers, axis=0, keepdims=True))
            dv = dot(probs.astype(BF16), gh, 1, 0)
            dprobs = dot(value[:, cols], gh, 1, 1)
            inner = jnp.sum(probs * dprobs, axis=0, keepdims=True)
            dscores = (probs * (dprobs - inner)).astype(BF16)
            dq = dot(dscores, kh, 0, 0)
            dqs[rows, cols] = (dq * (weight * scale)).astype(BF16)
            dvs[rows, cols] = (dv * weight).astype(BF16)
    for j, grads in enumerate((dqs, dvs)):
        for clip in range(2):
            rows = slice(clip * CLIP, (clip + 1) * CLIP)
            total = dot(grads[rows], ups[j], 1, 1)
            dlow[clip, j] = total if step == 0 else dlow_in[clip, j] + total
        store_pieces(gup, j, dot(low[j], grads[...], 0, 0))


def store_pieces(out, j, total):
    for piece in range(RANK // 8):
        part = total[piece * 8 : (piece + 1) * 8]
        part = jnp.concatenate(
            [part[:, h * HEAD : (h + 1) * HEAD] for h in range(LOCAL_HEADS)], axis=0
        )
        at = j * (RANK // 8) + piece
        out[at // NZ, at % NZ] = part.astype(BF16)


PIECES = (4, NZ, 40, 128)
LOWS = (2, 2, CLIP, RANK)


def attend(step, place, arrays, peer, up_own, up_other, *lows):
    def shard(place):
        return lax.rem(place[1] + step, NY)

    own_spec = pl.BlockSpec((CLIP, SHARD), lambda i, place: (0, place[0] * NY + shard(place)))
    peer_specs = [
        pl.BlockSpec((1, CLIP, SHARD), lambda i, place, n=n: (n, 0, shard(place)))
        for n in range(4)
    ]
    out_shape = [jax.ShapeDtypeStruct(PIECES, BF16), jax.ShapeDtypeStruct(LOWS, F32)]
    if step == 0:
        out_shape += [
            jax.ShapeDtypeStruct((2, 2 * CLIP, RANK), BF16),
            jax.ShapeDtypeStruct((2, 8, RANK), F32),
        ]
    return pl.pallas_call(
        functools.partial(attend_kernel, step),
        grid_spec=pltpu.PrefetchScalarGridSpec(
            num_scalar_prefetch=1,
            grid=(1,),
            in_specs=[own_spec] * 4
            + peer_specs
            + [whole(a.shape) for a in (up_own, up_other, *lows)],
            out_specs=[whole(a.shape) for a in out_shape],
            scratch_shapes=[
                pltpu.VMEM((2, RANK, SHARD), BF16),
                pltpu.VMEM((2 * CLIP, SHARD), BF16),
                pltpu.VMEM((2 * CLIP, SHARD), BF16),
            ],
        ),
        out_shape=out_shape,
        compiler_params=pltpu.CompilerParams(vmem_limit_bytes=24 * 1024 * 1024),
        cost_estimate=pl.CostEstimate(
            flops=4000000000, bytes_accessed=3000000, transcendentals=400000
        ),
        name="attend",
    )(place, *arrays, peer, peer, peer, peer, up_own, up_other, *lows)


def down_kernel(place, n0, n1, mine, peer, *refs):
    outs, dlow = refs[:NY], refs[NY]

    @pl.when(pl.program_id(0) == 0)
    def _():
        for j in range(2):
            for clip in range(2):
                total = mine[clip, j] + peer[1 - clip, j]
                dlow[j * RANK : (j + 1) * RANK, clip * CLIP : (clip + 1) * CLIP] = total.astype(
                    BF16
                ).T

    normed = jnp.concatenate([n0[...], n1[0]], axis=0)
    total = dot(dlow[...], normed, 1, 0)
    for step in range(NY):

        @pl.when(pl.program_id(0) == step)
        def _(out=outs[step]):
            for j in range(2):
                store_pieces(out, j, total[j * RANK : (j + 1) * RANK])


def down_grads(place, nown, peer, mine, theirs):
    def shard(i, place):
        return lax.rem(place[1] + i, NY)

    return pl.pallas_call(
        down_kernel,
        grid_spec=pltpu.PrefetchScalarGridSpec(
            num_scalar_prefetch=1,
            grid=(NY,),
            in_specs=[
                pl.BlockSpec((CLIP, SHARD), lambda i, place: (0, shard(i, place))),
                pl.BlockSpec((1, CLIP, SHARD), lambda i, place: (4, 0, shard(i, place))),
                whole(LOWS),
                whole(LOWS),
            ],
            out_specs=[whole(PIECES)] * NY,
            scratch_shapes=[pltpu.VMEM((2 * RANK, 2 * CLIP), BF16)],
        ),
        out_shape=[jax.ShapeDtypeStruct(PIECES, BF16)] * NY,
        compiler_params=pltpu.CompilerParams(vmem_limit_bytes=24 * 1024 * 1024),
        cost_estimate=pl.CostEstimate(
            flops=3000000000, bytes_accessed=5000000, transcendentals=0
        ),
        name="down_grads",
    )(place, nown, peer, mine, theirs)


def sum_y_kernel(place, *refs):
    ups, downs, outs = refs[:4], refs[4:8], refs[8:]
    x = place[3]
    for quarter in range(4):
        source = lax.rem(quarter + x, 4)
        for z in range(NZ):
            up = sum(r[source, z].astype(F32) for r in ups)
            down = sum(r[source, z].astype(F32) for r in downs)
            outs[quarter][z] = jnp.concatenate([up, down], axis=0).astype(BF16)


def sum_y(place, ups, downs):
    return pl.pallas_call(
        sum_y_kernel,
        out_shape=[jax.ShapeDtypeStruct((NZ, 80, 128), BF16)] * 4,
        in_specs=[pl.BlockSpec(memory_space=pltpu.SMEM)]
        + [pl.BlockSpec(memory_space=pltpu.VMEM)] * 8,
        out_specs=[pl.BlockSpec(memory_space=pltpu.VMEM)] * 4,
        compiler_params=pltpu.CompilerParams(vmem_limit_bytes=VMEM_LIMIT),
        name="sum_y",
    )(place, *ups, *downs)


def finish_kernel(factor, place, own, first, second, first_peer, second_peer, down, up, flat):
    core, x = place[2], place[3]

    def write(step, ref):
        quarter = lax.rem(x + step, 4)
        for z in range(NZ):
            part = ref[z].astype(F32) * factor
            for out, begin in ((up, 0), (flat, 40)):
                out[quarter * NZ + z] = jnp.concatenate(
                    [part[begin + h * 8 : begin + (h + 1) * 8] for h in range(LOCAL_HEADS)], axis=1
                )

    @pl.when(core == 0)
    def _():
        for step, ref in enumerate((own, second, first_peer, first)):
            write(step, ref)

    @pl.when(core == 1)
    def _():
        for step, ref in enumerate((second, second_peer, first, first_peer)):
            write(step, ref)

    for j in range(2):
        rows = flat[j * 2 * NZ : (j + 1) * 2 * NZ].reshape(RANK, SHARD)
        down[j] = rows.T


def finish(factor, place, *parts):
    return pl.pallas_call(
        functools.partial(finish_kernel, factor),
        out_shape=(
            jax.ShapeDtypeStruct((2, SHARD, RANK), F32),
            jax.ShapeDtypeStruct((4 * NZ, 8, SHARD), F32),
        ),
        in_specs=[pl.BlockSpec(memory_space=pltpu.SMEM)]
        + [pl.BlockSpec(memory_space=pltpu.VMEM)] * 5,
        out_specs=(pl.BlockSpec(memory_space=pltpu.VMEM),) * 2,
        scratch_shapes=[pltpu.VMEM((4 * NZ, 8, SHARD), F32)],
        compiler_params=pltpu.CompilerParams(vmem_limit_bytes=VMEM_LIMIT),
        name="finish",
    )(place, *parts)


def cross_x(part):
    other = send(part, lambda x, y, z, c: (x - 1, y, z, 1) if c == 0 else (x, y, z, 0))
    own = send(part, lambda x, y, z, c: (x, y, z, 0) if c == 0 else (x + 1, y, z, 1))
    return own, other


def gather(part):
    first = cross_x(part[None])
    rest = cross_x(jnp.stack([send_y(part, -step) for step in range(1, NY)]))
    return first, rest


def local(states, steps, q, k, v, g, down_maps, up_maps):
    dp, fsdp = lax.axis_index("dp"), lax.axis_index("fsdp")
    core, x_lo, y = dp % 2, fsdp // NY, fsdp % NY
    x = (dp // (2 * NZ)) * 2 + x_lo
    place = jnp.stack([x_lo ^ core, y, core, x]).astype(jnp.int32)
    weight = (steps[0].astype(F32) + 1.0) / NSTEPS
    weight = jnp.full((8, RANK), weight, F32)

    down_part = lax.dynamic_index_in_dim(down_maps, core, 0, keepdims=False)
    up_part = lax.dynamic_index_in_dim(up_maps, core, 0, keepdims=False)
    down_first, down_rest = gather(down_part)
    nown, nsend = normalize(place, states, q, k, v, g)
    peer = swap_cores(nsend)
    up_first, up_rest = gather(up_part)

    low_mine = lower(place, nown, peer, *down_first, *down_rest, weight)
    low_peer = swap_cores(low_mine)
    rows = (place, (q, k, v, g), peer)
    gup, dlow, low, weights = attend(0, *rows, *up_first, low_mine, low_peer)
    ups = [gup]
    for step in range(1, NY):
        gup, dlow = attend(step, *rows, *up_rest, low, weights, dlow)
        ups.append(send_y(gup, step))
    downs = down_grads(place, nown, peer, dlow, swap_cores(dlow))
    downs = [downs[0]] + [send_y(downs[step], step) for step in range(1, NY)]

    quarters = sum_y(place, ups, downs)
    parts = [
        quarters[0],
        send(quarters[1], lambda x, y, z, c: (x + 1, y, z, 1 - c)),
        send(quarters[2], lambda x, y, z, c: (x + 2, y, z, c)),
        send(quarters[3], lambda x, y, z, c: (x - 1, y, z, 1 - c)),
    ]
    eighths = sum(part.astype(F32) for part in parts).astype(BF16)
    eighths = exchange_z(eighths)
    piece = jnp.sum(eighths.astype(F32), axis=0).astype(BF16)
    quarter = exchange_z(jnp.broadcast_to(piece, (NZ, 80, 128)))

    first = send(
        quarter, lambda x, y, z, c: (x + 2, y, z, 1) if c == 0 else (x + 1, y, z, 0)
    )
    second = send(
        quarter, lambda x, y, z, c: (x, y, z, 1) if c == 0 else (x - 1, y, z, 0)
    )
    first_peer = swap_cores(first)
    second_peer = swap_cores(second)
    data_count = lax.axis_size("dp") * lax.axis_size("fsdp")
    factor = 1.0 / math.sqrt(CLIP * data_count)
    grad_down, grad_up = finish(
        factor, place, quarter, first, second, first_peer, second_peer
    )
    return (grad_down, grad_up.reshape(2, RANK, SHARD))


def solution(mesh):
    in_specs = (
        P(("dp", "fsdp"), None),
        P(("dp", "fsdp")),
        P(("dp", "fsdp"), None),
        P(("dp", "fsdp"), None),
        P(("dp", "fsdp"), None),
        P(("dp", "fsdp"), None),
        P(None, "fsdp", None),
        P(None, None, "fsdp"),
    )
    out_specs = (P(None, "fsdp", None), P(None, None, "fsdp"))
    return jax.shard_map(local, mesh=mesh, in_specs=in_specs, out_specs=out_specs, check_vma=False)
```

```python
import functools
import math

import jax
import jax.numpy as jnp
from jax import lax
from jax.experimental import pallas as pl
from jax.experimental.pallas import tpu as pltpu
from jax.sharding import PartitionSpec as P

HEADS = 40
NSTEPS = 1000
AXES = ("dp", "fsdp")
NX, NY, NZ, NC = 4, 4, 8, 2
BF16 = jnp.bfloat16
F32 = jnp.float32

CLIP = 192
WIDTH = 5120
HALF = WIDTH // 2
SHARD = 640
RANK = 128
HEAD = 128
LOCAL_HEADS = SHARD // HEAD
NORM_ROWS = 32
VMEM_LIMIT = 24 * 1024 * 1024
SMALL = pl.CostEstimate(flops=1000, bytes_accessed=1000, transcendentals=0)


def linear(x, y, z, c):
    x, y, z, c = x % NX, y % NY, z % NZ, c % NC
    return (((x // 2) * NZ + z) * NC + c) * 8 + (x % 2) * NY + y


def permutation(target):
    pairs = []
    for x in range(NX):
        for y in range(NY):
            for z in range(NZ):
                for c in range(NC):
                    pairs.append((linear(x, y, z, c), linear(*target(x, y, z, c))))
    return pairs


def send(value, target):
    return lax.ppermute(value, AXES, permutation(target))


def swap_cores(value):
    return send(value, lambda x, y, z, c: (x, y, z, 1 - c))


def send_y(value, step):
    return send(value, lambda x, y, z, c: (x, y + step, z, c))


Z_GROUPS = [
    [linear(x, y, z, c) for z in range(NZ)]
    for x in range(NX)
    for y in range(NY)
    for c in range(NC)
]


def scatter_x(parts):
    return [
        parts[0],
        send(parts[1], lambda x, y, z, c: (x + 1, y, z, 1 - c)),
        send(parts[2], lambda x, y, z, c: (x + 2, y, z, c)),
        send(parts[3], lambda x, y, z, c: (x - 1, y, z, 1 - c)),
    ]


def scatter_y(parts):
    return [parts[0]] + [send_y(parts[step], step) for step in range(1, NY)]


def exchange_z(value):
    return lax.all_to_all(value, AXES, 0, 0, axis_index_groups=Z_GROUPS, tiled=True)


def dot(a, b, ca, cb):
    return lax.dot_general(a, b, (((ca,), (cb,)), ((), ())), preferred_element_type=F32)


def whole(shape):
    return pl.BlockSpec(shape, lambda *_: (0,) * len(shape))


def normalize_kernel(place, states, q, k, v, g, nown, nsend):
    mine = pl.multiple_of(place[0] * HALF, HALF)
    other = pl.multiple_of((1 - place[0]) * HALF, HALF)
    for start in range(0, NORM_ROWS, 16):
        rows = slice(start, start + 16)
        inputs = states[rows, :].astype(F32)
        mean = jnp.mean(inputs, axis=1, keepdims=True)
        center = inputs - mean
        spread = jnp.mean(center * center, axis=1, keepdims=True)
        inverse = lax.rsqrt(spread + 1e-06)
        for begin, out in ((mine, nown), (other, nsend.at[4])):
            part = states[rows, pl.ds(begin, HALF)].astype(F32)
            out[rows, :] = ((part - mean) * inverse).astype(BF16)
    for n, src in enumerate((q, k, v, g)):
        nsend[n] = src[...]


def normalize(place, states, q, k, v, g):
    half = pl.BlockSpec((NORM_ROWS, HALF), lambda i, place: (i, 1 - place[0]))
    return pl.pallas_call(
        normalize_kernel,
        grid_spec=pltpu.PrefetchScalarGridSpec(
            num_scalar_prefetch=1,
            grid=(CLIP // NORM_ROWS,),
            in_specs=[pl.BlockSpec((NORM_ROWS, WIDTH), lambda i, place: (i, 0))] + [half] * 4,
            out_specs=(
                pl.BlockSpec((NORM_ROWS, HALF), lambda i, place: (i, 0)),
                pl.BlockSpec((5, NORM_ROWS, HALF), lambda i, place: (0, i, 0)),
            ),
        ),
        out_shape=(
            jax.ShapeDtypeStruct((CLIP, HALF), BF16),
            jax.ShapeDtypeStruct((5, CLIP, HALF), BF16),
        ),
        compiler_params=pltpu.CompilerParams(vmem_limit_bytes=60 * 1024 * 1024),
        cost_estimate=SMALL,
        name="normalize",
    )(place, states, q, k, v, g)


def lower_kernel(place, nown, npeer, own, other, weight, out0, out1):
    core, y = place[2], place[1]
    for clip in range(2):
        totals = [jnp.zeros((CLIP, RANK), F32) for _ in range(2)]
        for step in range(NY):
            start = pl.multiple_of(lax.rem(y + step, NY) * SHARD, SHARD)
            if clip == 0:
                rows = nown[:, pl.ds(start, SHARD)]
            else:
                rows = npeer[0, :, pl.ds(start, SHARD)]
            totals[0] += dot(rows, own[step], 1, 0)
            totals[1] += dot(rows, other[step], 1, 0)
        out = (out0, out1)[clip]
        out[core, :CLIP] = totals[0]
        out[1 - core, :CLIP] = totals[1]
        out[0, CLIP:] = weight[...]
        out[1, CLIP:] = weight[...]


def lower(place, nown, peer, *downs_and_weight):
    return pl.pallas_call(
        lower_kernel,
        grid=(1,),
        out_shape=[jax.ShapeDtypeStruct((2, CLIP + 8, RANK), F32)] * 2,
        in_specs=[
            pl.BlockSpec(memory_space=pltpu.SMEM),
            whole((CLIP, HALF)),
            pl.BlockSpec((1, CLIP, HALF), lambda i: (4, 0, 0)),
        ]
        + [whole(a.shape) for a in downs_and_weight],
        out_specs=[whole((2, CLIP + 8, RANK))] * 2,
        compiler_params=pltpu.CompilerParams(vmem_limit_bytes=VMEM_LIMIT),
        name="lower",
    )(place, nown, peer, *downs_and_weight)


def attend_kernel(first, after, place, *refs):
    q0, k0, v0, g0, q1, k1, v1, g1, up = refs[:9]
    refs = refs[9 + after :]
    if first:
        mine0, mine1, peer0, peer1, gup, dlow0, dlow1, low, weights, ups, dqs, dvs = refs
        for j in range(2):
            for clip in range(2):
                total = (mine0, mine1)[clip][j, :CLIP] + (peer1, peer0)[clip][j, :CLIP]
                low[j, clip * CLIP : (clip + 1) * CLIP] = total.astype(BF16)
        weights[0] = mine0[0, CLIP:]
        weights[1] = peer0[0, CLIP:]
    else:
        low, weights, in0, in1, gup, dlow0, dlow1, ups, dqs, dvs = refs
    core = place[2]
    scale = 1.0 / math.sqrt(HEAD)
    ups[core] = up[0]
    ups[1 - core] = up[1]
    for clip in range(2):
        rows = slice(clip * CLIP, (clip + 1) * CLIP)
        weight = weights[clip, :1]
        if clip == 0:
            q, k, v, g = (r[...] for r in (q0, k0, v0, g0))
        else:
            q, k, v, g = (r[0] for r in (q1, k1, v1, g1))
        query = (q.astype(F32) + dot(low[0, rows], ups[0], 1, 0)).astype(BF16)
        value = (v.astype(F32) + dot(low[1, rows], ups[1], 1, 0)).astype(BF16)
        for h in range(LOCAL_HEADS):
            cols = slice(h * HEAD, (h + 1) * HEAD)
            kh, gh = k[:, cols], g[:, cols]
            scores = dot(kh, query[:, cols], 1, 1) * scale
            powers = jnp.exp(scores - jnp.max(scores, axis=0, keepdims=True))
            probs = powers * (1.0 / jnp.sum(powers, axis=0, keepdims=True))
            dv = dot(probs.astype(BF16), gh, 1, 0)
            dprobs = dot(value[:, cols], gh, 1, 1)
            inner = jnp.sum(probs * dprobs, axis=0, keepdims=True)
            dscores = (probs * (dprobs - inner)).astype(BF16)
            dq = dot(dscores, kh, 0, 0)
            dqs[rows, cols] = (dq * (weight * scale)).astype(BF16)
            dvs[rows, cols] = (dv * weight).astype(BF16)
    for j, grads in enumerate((dqs, dvs)):
        for clip in range(2):
            rows = slice(clip * CLIP, (clip + 1) * CLIP)
            total = dot(grads[rows], ups[j], 1, 1)
            out = (dlow0, dlow1)[clip]
            out[j] = total if first else (in0, in1)[clip][j] + total
        store_pieces(gup, j, dot(low[j], grads[...], 0, 0))


def lane_blocks(rows):
    return jnp.concatenate(
        [rows[:, h * HEAD : (h + 1) * HEAD] for h in range(LOCAL_HEADS)], axis=0
    )


def store_pieces(out, j, total):
    for piece in range(RANK // 8):
        at = j * (RANK // 8) + piece
        out[at // NZ, at % NZ] = lane_blocks(total[piece * 8 : (piece + 1) * 8]).astype(BF16)


PIECES = (4, NZ, 40, 128)
LOWS = (2, CLIP, RANK)


def attend(step, after, place, arrays, peer, ups, *lows):
    def shard(place):
        return lax.rem(place[1] + step, NY)

    own_spec = pl.BlockSpec((CLIP, SHARD), lambda i, place: (0, place[0] * NY + shard(place)))
    peer_specs = [
        pl.BlockSpec((1, CLIP, SHARD), lambda i, place, n=n: (n, 0, shard(place)))
        for n in range(4)
    ]
    out_shape = [jax.ShapeDtypeStruct(PIECES, BF16)] + [jax.ShapeDtypeStruct(LOWS, F32)] * 2
    first = step == 0
    if first:
        out_shape += [
            jax.ShapeDtypeStruct((2, 2 * CLIP, RANK), BF16),
            jax.ShapeDtypeStruct((2, 8, RANK), F32),
        ]
    return pl.pallas_call(
        functools.partial(attend_kernel, first, len(after)),
        grid_spec=pltpu.PrefetchScalarGridSpec(
            num_scalar_prefetch=1,
            grid=(1,),
            in_specs=[own_spec] * 4
            + peer_specs
            + [whole((2, RANK, SHARD))]
            + [pl.BlockSpec(memory_space=pl.ANY)] * len(after)
            + [whole(a.shape) for a in lows],
            out_specs=[whole(a.shape) for a in out_shape],
            scratch_shapes=[
                pltpu.VMEM((2, RANK, SHARD), BF16),
                pltpu.VMEM((2 * CLIP, SHARD), BF16),
                pltpu.VMEM((2 * CLIP, SHARD), BF16),
            ],
        ),
        out_shape=out_shape,
        compiler_params=pltpu.CompilerParams(vmem_limit_bytes=24 * 1024 * 1024),
        cost_estimate=SMALL,
        name="attend",
    )(place, *arrays, peer, peer, peer, peer, ups[step], *after, *lows)


def down_kernel(after, place, n0, n1, mine0, mine1, peer0, peer1, *refs):
    *outs, dlow, totals = refs[after:]

    @pl.when(pl.program_id(0) == 0)
    def _():
        for j in range(2):
            for clip in range(2):
                total = (mine0, mine1)[clip][j] + (peer1, peer0)[clip][j]
                dlow[j * RANK : (j + 1) * RANK, clip * CLIP : (clip + 1) * CLIP] = total.astype(
                    BF16
                ).T

    normed = jnp.concatenate([n0[...], n1[0]], axis=0)
    totals[...] = dot(dlow[...], normed, 1, 0)
    for step, out in enumerate(outs):
        first = lax.rem(place[3] + step, NX) * (2 * RANK // NX)
        for z in range(NZ):
            rows = totals[pl.ds(pl.multiple_of(first + z * 8, 8), 8), :]
            out[0, z] = lane_blocks(rows).astype(BF16)


def down_grads(place, nown, peer, dlows, *after):
    return pl.pallas_call(
        functools.partial(down_kernel, len(after)),
        grid_spec=pltpu.PrefetchScalarGridSpec(
            num_scalar_prefetch=1,
            grid=(NY,),
            in_specs=[
                pl.BlockSpec((CLIP, SHARD), lambda i, place: (0, lax.rem(place[1] + i, NY))),
                pl.BlockSpec(
                    (1, CLIP, SHARD), lambda i, place: (4, 0, lax.rem(place[1] + i, NY))
                ),
            ]
            + [whole(LOWS)] * 4
            + [pl.BlockSpec(memory_space=pl.ANY)] * len(after),
            out_specs=[pl.BlockSpec((1, *PIECES[1:]), lambda i, place: (i, 0, 0, 0))] * NX,
            scratch_shapes=[
                pltpu.VMEM((2 * RANK, 2 * CLIP), BF16),
                pltpu.VMEM((2 * RANK, SHARD), F32),
            ],
        ),
        out_shape=[jax.ShapeDtypeStruct((NY, *PIECES[1:]), BF16)] * NX,
        compiler_params=pltpu.CompilerParams(vmem_limit_bytes=24 * 1024 * 1024),
        cost_estimate=SMALL,
        name="down_grads",
    )(place, nown, peer, *dlows, *after)


def sum_y_kernel(place, *refs):
    parts, outs = refs[:4], refs[4:]
    x = place[3]
    for quarter in range(4):
        source = lax.rem(quarter + x, 4)
        for z in range(NZ):
            total = sum(r[source, z].astype(F32) for r in parts)
            outs[quarter][z] = total.astype(BF16)


def sum_y(place, parts):
    return pl.pallas_call(
        sum_y_kernel,
        out_shape=[jax.ShapeDtypeStruct(PIECES[1:], BF16)] * 4,
        in_specs=[pl.BlockSpec(memory_space=pltpu.SMEM)]
        + [pl.BlockSpec(memory_space=pltpu.VMEM)] * 4,
        out_specs=[pl.BlockSpec(memory_space=pltpu.VMEM)] * 4,
        compiler_params=pltpu.CompilerParams(vmem_limit_bytes=VMEM_LIMIT),
        cost_estimate=SMALL,
        name="sum_y",
    )(place, *parts)


def sum_x_kernel(*refs):
    parts, outs = refs[:4], refs[4:]
    for step in range(NY):
        outs[step][...] = sum(r[step].astype(F32) for r in parts).astype(BF16)


def sum_x(parts):
    return pl.pallas_call(
        sum_x_kernel,
        out_shape=[jax.ShapeDtypeStruct(PIECES[1:], BF16)] * NY,
        in_specs=[pl.BlockSpec(memory_space=pltpu.VMEM)] * 4,
        out_specs=[pl.BlockSpec(memory_space=pltpu.VMEM)] * NY,
        compiler_params=pltpu.CompilerParams(vmem_limit_bytes=VMEM_LIMIT),
        cost_estimate=SMALL,
        name="sum_x",
    )(*parts)


def join_kernel(*refs):
    ups, downs, out = refs[:4], refs[4:8], refs[8]
    for z in range(NZ):
        up = sum(r[z].astype(F32) for r in ups)
        down = sum(r[z].astype(F32) for r in downs)
        out[z] = jnp.concatenate([up, down], axis=0).astype(BF16)


def join(ups, downs):
    return pl.pallas_call(
        join_kernel,
        out_shape=jax.ShapeDtypeStruct((NZ, 80, 128), BF16),
        in_specs=[pl.BlockSpec(memory_space=pltpu.VMEM)] * 8,
        out_specs=pl.BlockSpec(memory_space=pltpu.VMEM),
        compiler_params=pltpu.CompilerParams(vmem_limit_bytes=VMEM_LIMIT),
        cost_estimate=SMALL,
        name="join",
    )(*ups, *downs)


def finish_kernel(factor, place, own, first, second, first_peer, second_peer, down, up, flat):
    core, x = place[2], place[3]

    def write(step, ref):
        quarter = lax.rem(x + step, 4)
        for z in range(NZ):
            part = ref[z].astype(F32) * factor
            for out, begin in ((up, 0), (flat, 40)):
                out[quarter * NZ + z] = jnp.concatenate(
                    [part[begin + h * 8 : begin + (h + 1) * 8] for h in range(LOCAL_HEADS)], axis=1
                )

    @pl.when(core == 0)
    def _():
        for step, ref in enumerate((own, second, first_peer, first)):
            write(step, ref)

    @pl.when(core == 1)
    def _():
        for step, ref in enumerate((second, second_peer, first, first_peer)):
            write(step, ref)

    for j in range(2):
        rows = flat[j * 2 * NZ : (j + 1) * 2 * NZ].reshape(RANK, SHARD)
        down[j] = rows.T


def finish(factor, place, *parts):
    return pl.pallas_call(
        functools.partial(finish_kernel, factor),
        out_shape=(
            jax.ShapeDtypeStruct((2, SHARD, RANK), F32),
            jax.ShapeDtypeStruct((4 * NZ, 8, SHARD), F32),
        ),
        in_specs=[pl.BlockSpec(memory_space=pltpu.SMEM)]
        + [pl.BlockSpec(memory_space=pltpu.VMEM)] * 5,
        out_specs=(pl.BlockSpec(memory_space=pltpu.VMEM),) * 2,
        scratch_shapes=[pltpu.VMEM((4 * NZ, 8, SHARD), F32)],
        compiler_params=pltpu.CompilerParams(vmem_limit_bytes=VMEM_LIMIT),
        name="finish",
    )(place, *parts)


def cross_x(part):
    other = send(part, lambda x, y, z, c: (x - 1, y, z, 1) if c == 0 else (x, y, z, 0))
    own = send(part, lambda x, y, z, c: (x, y, z, 0) if c == 0 else (x + 1, y, z, 1))
    return own, other


def local(states, steps, q, k, v, g, down_maps, up_maps):
    dp, fsdp = lax.axis_index("dp"), lax.axis_index("fsdp")
    core, x_lo, y = dp % 2, fsdp // NY, fsdp % NY
    x = (dp // (2 * NZ)) * 2 + x_lo
    place = jnp.stack([x_lo ^ core, y, core, x]).astype(jnp.int32)
    weight = (steps[0].astype(F32) + 1.0) / NSTEPS
    weight = jnp.full((8, RANK), weight, F32)

    down_part = lax.dynamic_index_in_dim(down_maps, core, 0, keepdims=False)
    up_part = lax.dynamic_index_in_dim(up_maps, core, 0, keepdims=False)
    nown, nsend = normalize(place, states, q, k, v, g)
    downs = [send_y(down_part, -step) for step in range(1, NY)]
    up = jnp.stack(cross_x(up_part))
    nsend, up, *downs = lax.optimization_barrier((nsend, up, *downs))
    downs = cross_x(jnp.stack([down_part, *downs]))
    ups = [up] + [send_y(up, -step) for step in range(1, NY)]
    peer = swap_cores(nsend)

    lows = lower(place, nown, peer, *downs, weight)
    lows = [*lows, *(swap_cores(part) for part in lows)]
    rows = (place, (q, k, v, g), peer, ups)
    gups = [None] * NY
    gups[0], *dlow, low, weights = attend(0, (), *rows, *lows)
    gup, *dlow = attend(1, (), *rows, low, weights, *dlow)
    gups[1] = send_y(gup, 1)
    gup, *dlow = attend(3, (), *rows, low, weights, *dlow)
    gups[3] = send_y(gup, 3)
    gup, *dlow = attend(2, (), *rows, low, weights, *dlow)
    gups[2] = send_y(gup, 2)
    dlows = [*dlow, *(swap_cores(part) for part in dlow)]
    gdowns = scatter_x(down_grads(place, nown, peer, dlows, gups[1]))
    ups = scatter_x(sum_y(place, gups))
    downs = scatter_y(sum_x(gdowns))
    eighths = join(ups, downs)
    eighths = exchange_z(eighths)
    piece = jnp.sum(eighths.astype(F32), axis=0).astype(BF16)
    quarter = exchange_z(jnp.broadcast_to(piece, (NZ, 80, 128)))

    first = send(
        quarter, lambda x, y, z, c: (x + 2, y, z, 1) if c == 0 else (x + 1, y, z, 0)
    )
    second = send(
        quarter, lambda x, y, z, c: (x, y, z, 1) if c == 0 else (x - 1, y, z, 0)
    )
    first_peer = swap_cores(first)
    second_peer = swap_cores(second)
    data_count = lax.axis_size("dp") * lax.axis_size("fsdp")
    factor = 1.0 / math.sqrt(CLIP * data_count)
    grad_down, grad_up = finish(
        factor, place, quarter, first, second, first_peer, second_peer
    )
    return (grad_down, grad_up.reshape(2, RANK, SHARD))


def solution(mesh):
    in_specs = (
        P(("dp", "fsdp"), None),
        P(("dp", "fsdp")),
        P(("dp", "fsdp"), None),
        P(("dp", "fsdp"), None),
        P(("dp", "fsdp"), None),
        P(("dp", "fsdp"), None),
        P(None, "fsdp", None),
        P(None, None, "fsdp"),
    )
    out_specs = (P(None, "fsdp", None), P(None, None, "fsdp"))
    return jax.shard_map(local, mesh=mesh, in_specs=in_specs, out_specs=out_specs, check_vma=False)
```

```python
import functools
import math

import jax
import jax.numpy as jnp
from jax import lax
from jax.experimental import pallas as pl
from jax.experimental.pallas import tpu as pltpu
from jax.sharding import PartitionSpec as P

HEADS = 40
NSTEPS = 1000
AXES = ("dp", "fsdp")
NX, NY, NZ, NC = 4, 4, 8, 2
BF16 = jnp.bfloat16
F32 = jnp.float32
NORM_CHUNKS = 4
LOG2E = math.log2(math.e)

CLIP = 192
WIDTH = 5120
HALF = WIDTH // 2
SHARD = 640
RANK = 128
HEAD = 128
LOCAL_HEADS = SHARD // HEAD
VMEM_LIMIT = 24 * 1024 * 1024
SMALL = pl.CostEstimate(flops=1000, bytes_accessed=1000, transcendentals=0)


def linear(x, y, z, c):
    x, y, z, c = x % NX, y % NY, z % NZ, c % NC
    return (((x // 2) * NZ + z) * NC + c) * 8 + (x % 2) * NY + y


def permutation(target):
    pairs = []
    for x in range(NX):
        for y in range(NY):
            for z in range(NZ):
                for c in range(NC):
                    pairs.append((linear(x, y, z, c), linear(*target(x, y, z, c))))
    return pairs


def send(value, target):
    return lax.ppermute(value, AXES, permutation(target))


def swap_cores(value):
    return send(value, lambda x, y, z, c: (x, y, z, 1 - c))


def send_y(value, step):
    return send(value, lambda x, y, z, c: (x, y + step, z, c))


Z_GROUPS = [
    [linear(x, y, z, c) for z in range(NZ)]
    for x in range(NX)
    for y in range(NY)
    for c in range(NC)
]


def scatter_x(parts):
    return [
        parts[0],
        send(parts[1], lambda x, y, z, c: (x + 1, y, z, 1 - c)),
        send(parts[2], lambda x, y, z, c: (x + 2, y, z, c)),
        send(parts[3], lambda x, y, z, c: (x - 1, y, z, 1 - c)),
    ]


def scatter_y(parts):
    return [parts[0]] + [send_y(parts[step], step) for step in range(1, NY)]


def exchange_z(value):
    return lax.all_to_all(value, AXES, 0, 0, axis_index_groups=Z_GROUPS, tiled=True)


def dot(a, b, ca, cb):
    return lax.dot_general(a, b, (((ca,), (cb,)), ((), ())), preferred_element_type=F32)


def whole(shape):
    return pl.BlockSpec(shape, lambda *_: (0,) * len(shape))


SCALARS = pl.BlockSpec(memory_space=pltpu.SMEM)
RESIDENT = pl.BlockSpec(memory_space=pltpu.VMEM)
ANYWHERE = pl.BlockSpec(memory_space=pl.ANY)


def call(kernel, name, out_shape, scratch, place, resident, after=()):
    outs = [jax.ShapeDtypeStruct(shape, dtype) for shape, dtype in out_shape]
    return pl.pallas_call(
        kernel,
        out_shape=outs,
        in_specs=[SCALARS] + [RESIDENT] * len(resident) + [ANYWHERE] * len(after),
        out_specs=[RESIDENT] * len(outs),
        scratch_shapes=[pltpu.VMEM(shape, dtype) for shape, dtype in scratch],
        compiler_params=pltpu.CompilerParams(vmem_limit_bytes=VMEM_LIMIT),
        cost_estimate=SMALL,
        name=name,
    )(place, *resident, *after)


def normalize_kernel(place, states, q, k, v, g, nown, nsend, held, sems):
    mine = pl.multiple_of(place[0] * HALF, HALF)
    other = pl.multiple_of((1 - place[0]) * HALF, HALF)
    size = CLIP // NORM_CHUNKS
    chunks = [
        pltpu.make_async_copy(
            states.at[pl.ds(n * size, size)], held.at[pl.ds(n * size, size)], sems.at[n]
        )
        for n in range(NORM_CHUNKS)
    ]
    copies = [
        pltpu.make_async_copy(
            src.at[:, pl.ds(other, HALF)], nsend.at[n], sems.at[NORM_CHUNKS + n]
        )
        for n, src in enumerate((q, k, v, g))
    ]
    for copy in chunks + copies:
        copy.start()

    def block(step, carry):
        rows = pl.ds(pl.multiple_of(step * 16, 16), 16)
        inputs = held[rows, :].astype(F32)
        mean = jnp.mean(inputs, axis=1, keepdims=True)
        center = inputs - mean
        spread = jnp.mean(center * center, axis=1, keepdims=True)
        inverse = lax.rsqrt(spread + 1e-06)
        for begin, out in ((mine, nown), (other, nsend.at[4])):
            part = held[rows, pl.ds(begin, HALF)].astype(F32)
            out[rows, :] = ((part - mean) * inverse).astype(BF16)
        return carry

    for n, copy in enumerate(chunks):
        copy.wait()
        lax.fori_loop(n * size // 16, (n + 1) * size // 16, block, 0)
    for copy in copies:
        copy.wait()


def normalize(place, *arrays):
    return pl.pallas_call(
        normalize_kernel,
        out_shape=[
            jax.ShapeDtypeStruct((CLIP, HALF), BF16),
            jax.ShapeDtypeStruct((5, CLIP, HALF), BF16),
        ],
        in_specs=[SCALARS] + [pl.BlockSpec(memory_space=pl.ANY)] * 5,
        out_specs=[RESIDENT] * 2,
        scratch_shapes=[
            pltpu.VMEM((CLIP, WIDTH), BF16),
            pltpu.SemaphoreType.DMA((NORM_CHUNKS + 4,)),
        ],
        compiler_params=pltpu.CompilerParams(vmem_limit_bytes=VMEM_LIMIT),
        cost_estimate=SMALL,
        name="normalize",
    )(place, *(pltpu.with_memory_space_constraint(array, pltpu.HBM) for array in arrays))


def lower_kernel(place, nown, npeer, own, other, weight, out0, out1):
    core, y = place[2], place[1]
    total = jnp.zeros((2 * CLIP, 2 * RANK), F32)
    for step in range(NY):
        at = pl.ds(pl.multiple_of(lax.rem(y + step, NY) * SHARD, SHARD), SHARD)
        rows = jnp.concatenate([nown[:, at], npeer[4, :, at]], axis=0)
        total += dot(rows, jnp.concatenate([own[step], other[step]], axis=1), 1, 0)
    for clip, out in enumerate((out0, out1)):
        out[core, :CLIP] = total[clip * CLIP : (clip + 1) * CLIP, :RANK]
        out[1 - core, :CLIP] = total[clip * CLIP : (clip + 1) * CLIP, RANK:]
        out[0, CLIP:] = weight[...]
        out[1, CLIP:] = weight[...]


def lower(place, *arrays):
    return call(lower_kernel, "lower", [((2, CLIP + 8, RANK), F32)] * 2, [], place, arrays)


def attend_kernel(steps, first, after, place, *refs):
    count = len(steps)
    own, peer, lows, given = refs[:4], refs[4], refs[5:9], refs[9 : 9 + count]
    refs = refs[9 + count + after :]
    gups, dlow0, dlow1, rest = refs[:count], refs[count], refs[count + 1], refs[count + 2 :]
    if first:
        mine0, mine1, peer0, peer1 = lows
        low, weights, ups, dqs, dvs = rest
        for j in range(2):
            for clip in range(2):
                total = (mine0, mine1)[clip][j, :CLIP] + (peer1, peer0)[clip][j, :CLIP]
                low[j, clip * CLIP : (clip + 1) * CLIP] = total.astype(BF16)
        weights[0] = mine0[0, CLIP:]
        weights[1] = peer0[0, CLIP:]
    else:
        low, weights, in0, in1 = lows
        ups, dqs, dvs = rest
    core = place[2]
    scale = 1.0 / math.sqrt(HEAD)
    clips = [slice(clip * CLIP, (clip + 1) * CLIP) for clip in range(2)]

    def load(n, clip):
        shard = lax.rem(place[1] + steps[n], NY) * SHARD
        if clip == 0:
            at = pl.ds(pl.multiple_of(place[0] * HALF + shard, SHARD), SHARD)
            q, k, v, g = (r[:, at] for r in own)
        else:
            at = pl.ds(pl.multiple_of(shard, SHARD), SHARD)
            q, k, v, g = (peer[m, :, at] for m in range(4))
        rows = clips[clip]
        query = (q.astype(F32) + dot(low[0, rows], ups[n, 0], 1, 0)).astype(BF16)
        value = (v.astype(F32) + dot(low[1, rows], ups[n, 1], 1, 0)).astype(BF16)
        for h in range(LOCAL_HEADS):
            cols = slice(h * HEAD, (h + 1) * HEAD)
            heads.append((n, clip, cols, query[:, cols], k[:, cols], value[:, cols], g[:, cols]))

    def products(head):
        query, key, value, grad = head[3:]
        return dot(key, query, 1, 1), dot(value, grad, 1, 1)

    def finish(head, probs, dscores):
        n, clip, cols, query, key, value, grad = head
        weight = weights[clip, :1]
        dvs[n, clips[clip], cols] = (dot(probs, grad, 1, 0) * weight).astype(BF16)
        dqs[n, clips[clip], cols] = (dot(dscores, key, 0, 0) * (weight * scale)).astype(BF16)

    def collect(n):
        for j, grads in enumerate((dqs, dvs)):
            for clip, out in enumerate((dlow0, dlow1)):
                total = dot(grads[n, clips[clip]], ups[n, j], 1, 1)
                if n == 0:
                    out[j] = total if first else (in0, in1)[clip][j] + total
                else:
                    out[j] += total
            store_pieces(gups[n], j, dot(low[j], grads[n], 0, 0))

    heads = []
    for n in range(count):
        ups[n, core] = given[n][0]
        ups[n, 1 - core] = given[n][1]
        for clip in range(2):
            load(n, clip)

    ready = products(heads[0])
    done = None
    for at, head in enumerate(heads):
        scores, dprobs = ready
        if at + 1 < len(heads):
            ready = products(heads[at + 1])
        if done is not None:
            finish(*done)
            if head[0] != done[0][0]:
                collect(done[0][0])
        top = jnp.max(scores, axis=0, keepdims=True)
        powers = jnp.exp2((scores - top) * (scale * LOG2E))
        probs = powers * (1.0 / jnp.sum(powers, axis=0, keepdims=True))
        inner = jnp.sum(probs * dprobs, axis=0, keepdims=True)
        done = (head, probs.astype(BF16), (probs * (dprobs - inner)).astype(BF16))
    finish(*done)
    collect(count - 1)


def lane_blocks(rows):
    return jnp.concatenate(
        [rows[:, h * HEAD : (h + 1) * HEAD] for h in range(LOCAL_HEADS)], axis=0
    )


def store_pieces(out, j, total):
    for piece in range(RANK // 8):
        at = j * (RANK // 8) + piece
        out[at // NZ, at % NZ] = lane_blocks(total[piece * 8 : (piece + 1) * 8]).astype(BF16)


PIECES = (4, NZ, 40, 128)
LOWS = (2, CLIP, RANK)


def attend(steps, after, place, arrays, peer, ups, *lows):
    first, count = lows[0].dtype == F32, len(steps)
    shapes = [(PIECES, BF16)] * count + [(LOWS, F32)] * 2
    if first:
        shapes += [((2, 2 * CLIP, RANK), BF16), ((2, 8, RANK), F32)]
    scratch = [((count, 2, RANK, SHARD), BF16)] + [((count, 2 * CLIP, SHARD), BF16)] * 2
    kernel = functools.partial(attend_kernel, steps, first, len(after))
    given = [ups[step] for step in steps]
    return call(
        kernel, "attend", shapes, scratch, place, (*arrays, peer, *lows, *given), after
    )


def down_kernel(after, place, nown, peer, mine0, mine1, peer0, peer1, *refs):
    *outs, dlow, totals = refs[after:]
    for j in range(2):
        for clip in range(2):
            total = (mine0, mine1)[clip][j] + (peer1, peer0)[clip][j]
            dlow[j * RANK : (j + 1) * RANK, clip * CLIP : (clip + 1) * CLIP] = total.astype(BF16).T
    for shift in range(NY):
        shard = pl.multiple_of(lax.rem(place[1] + shift, NY) * SHARD, SHARD)
        normed = jnp.concatenate([nown[:, pl.ds(shard, SHARD)], peer[4, :, pl.ds(shard, SHARD)]], axis=0)
        totals[shift] = dot(dlow[...], normed, 1, 0)
        for step, out in enumerate(outs):
            first = lax.rem(place[3] + step, NX) * (2 * RANK // NX)
            for z in range(NZ):
                rows = totals[shift, pl.ds(pl.multiple_of(first + z * 8, 8), 8), :]
                out[shift, z] = lane_blocks(rows).astype(BF16)


def down_grads(place, nown, peer, dlows, *after):
    shapes = [((NY, *PIECES[1:]), BF16)] * NX
    scratch = [((2 * RANK, 2 * CLIP), BF16), ((NY, 2 * RANK, SHARD), F32)]
    kernel = functools.partial(down_kernel, len(after))
    return call(kernel, "down_grads", shapes, scratch, place, (nown, peer, *dlows), after)


def sum_y_kernel(place, *refs):
    parts, outs = refs[:4], refs[4:]
    x = place[3]
    for quarter in range(4):
        source = lax.rem(quarter + x, 4)
        for z in range(NZ):
            total = sum(r[source, z].astype(F32) for r in parts)
            outs[quarter][z] = total.astype(BF16)


def sum_y(place, parts):
    return pl.pallas_call(
        sum_y_kernel,
        out_shape=[jax.ShapeDtypeStruct(PIECES[1:], BF16)] * 4,
        in_specs=[pl.BlockSpec(memory_space=pltpu.SMEM)]
        + [pl.BlockSpec(memory_space=pltpu.VMEM)] * 4,
        out_specs=[pl.BlockSpec(memory_space=pltpu.VMEM)] * 4,
        compiler_params=pltpu.CompilerParams(vmem_limit_bytes=VMEM_LIMIT),
        cost_estimate=SMALL,
        name="sum_y",
    )(place, *parts)


def sum_x_kernel(*refs):
    parts, outs = refs[:4], refs[4:]
    for step in range(NY):
        outs[step][...] = sum(r[step].astype(F32) for r in parts).astype(BF16)


def sum_x(parts):
    return pl.pallas_call(
        sum_x_kernel,
        out_shape=[jax.ShapeDtypeStruct(PIECES[1:], BF16)] * NY,
        in_specs=[pl.BlockSpec(memory_space=pltpu.VMEM)] * 4,
        out_specs=[pl.BlockSpec(memory_space=pltpu.VMEM)] * NY,
        compiler_params=pltpu.CompilerParams(vmem_limit_bytes=VMEM_LIMIT),
        cost_estimate=SMALL,
        name="sum_x",
    )(*parts)


def join_kernel(*refs):
    ups, downs, out = refs[:4], refs[4:8], refs[8]
    for z in range(NZ):
        up = sum(r[z].astype(F32) for r in ups)
        down = sum(r[z].astype(F32) for r in downs)
        out[z] = jnp.concatenate([up, down], axis=0).astype(BF16)


def join(ups, downs):
    return pl.pallas_call(
        join_kernel,
        out_shape=jax.ShapeDtypeStruct((NZ, 80, 128), BF16),
        in_specs=[pl.BlockSpec(memory_space=pltpu.VMEM)] * 8,
        out_specs=pl.BlockSpec(memory_space=pltpu.VMEM),
        compiler_params=pltpu.CompilerParams(vmem_limit_bytes=VMEM_LIMIT),
        cost_estimate=SMALL,
        name="join",
    )(*ups, *downs)


def finish_kernel(factor, place, own, first, second, first_peer, second_peer, down, up, flat):
    core, x = place[2], place[3]

    def write(step, ref):
        quarter = lax.rem(x + step, 4)
        for z in range(NZ):
            part = ref[z].astype(F32) * factor
            for out, begin in ((up, 0), (flat, 40)):
                out[quarter * NZ + z] = jnp.concatenate(
                    [part[begin + h * 8 : begin + (h + 1) * 8] for h in range(LOCAL_HEADS)], axis=1
                )

    @pl.when(core == 0)
    def _():
        for step, ref in enumerate((own, second, first_peer, first)):
            write(step, ref)

    @pl.when(core == 1)
    def _():
        for step, ref in enumerate((second, second_peer, first, first_peer)):
            write(step, ref)

    for j in range(2):
        rows = flat[j * 2 * NZ : (j + 1) * 2 * NZ].reshape(RANK, SHARD)
        down[j] = rows.T


def finish(factor, place, *parts):
    return pl.pallas_call(
        functools.partial(finish_kernel, factor),
        out_shape=(
            jax.ShapeDtypeStruct((2, SHARD, RANK), F32),
            jax.ShapeDtypeStruct((4 * NZ, 8, SHARD), F32),
        ),
        in_specs=[pl.BlockSpec(memory_space=pltpu.SMEM)]
        + [pl.BlockSpec(memory_space=pltpu.VMEM)] * 5,
        out_specs=(pl.BlockSpec(memory_space=pltpu.VMEM),) * 2,
        scratch_shapes=[pltpu.VMEM((4 * NZ, 8, SHARD), F32)],
        compiler_params=pltpu.CompilerParams(vmem_limit_bytes=VMEM_LIMIT),
        name="finish",
    )(place, *parts)


def cross_x(part):
    other = send(part, lambda x, y, z, c: (x - 1, y, z, 1) if c == 0 else (x, y, z, 0))
    own = send(part, lambda x, y, z, c: (x, y, z, 0) if c == 0 else (x + 1, y, z, 1))
    return own, other


def local(states, steps, q, k, v, g, down_maps, up_maps):
    dp, fsdp = lax.axis_index("dp"), lax.axis_index("fsdp")
    core, x_lo, y = dp % 2, fsdp // NY, fsdp % NY
    x = (dp // (2 * NZ)) * 2 + x_lo
    place = jnp.stack([x_lo ^ core, y, core, x]).astype(jnp.int32)
    weight = (steps[0].astype(F32) + 1.0) / NSTEPS
    weight = jnp.full((8, RANK), weight, F32)

    down_part = lax.dynamic_index_in_dim(down_maps, core, 0, keepdims=False)
    up_part = lax.dynamic_index_in_dim(up_maps, core, 0, keepdims=False)
    nown, nsend = normalize(place, states, q, k, v, g)
    downs = [send_y(down_part, -step) for step in range(1, NY)]
    up = jnp.stack(cross_x(up_part))
    nsend, up, *downs = lax.optimization_barrier((nsend, up, *downs))
    downs = cross_x(jnp.stack([down_part, *downs]))
    ups = [up] + [send_y(up, -step) for step in range(1, NY)]
    peer = swap_cores(nsend)

    lows = lower(place, nown, peer, *downs, weight)
    lows = [*lows, *(swap_cores(part) for part in lows)]
    rows = (place, (q, k, v, g), peer, ups)
    gups = [None] * NY
    gups[1], gups[3], *dlow, low, weights = attend((1, 3), (), *rows, *lows)
    gups[1], gups[3] = send_y(gups[1], 1), send_y(gups[3], 3)
    gups[2], gups[0], *dlow = attend((2, 0), (), *rows, low, weights, *dlow)
    gups[2] = send_y(gups[2], 2)
    dlows = [*dlow, *(swap_cores(part) for part in dlow)]
    gdowns = scatter_x(down_grads(place, nown, peer, dlows, gups[1], gups[3]))
    ups = scatter_x(sum_y(place, gups))
    downs = scatter_y(sum_x(gdowns))
    eighths = join(ups, downs)
    eighths = exchange_z(eighths)
    piece = jnp.sum(eighths.astype(F32), axis=0).astype(BF16)
    quarter = exchange_z(jnp.broadcast_to(piece, (NZ, 80, 128)))

    first = send(
        quarter, lambda x, y, z, c: (x + 2, y, z, 1) if c == 0 else (x + 1, y, z, 0)
    )
    second = send(
        quarter, lambda x, y, z, c: (x, y, z, 1) if c == 0 else (x - 1, y, z, 0)
    )
    first_peer = swap_cores(first)
    second_peer = swap_cores(second)
    data_count = lax.axis_size("dp") * lax.axis_size("fsdp")
    factor = 1.0 / math.sqrt(CLIP * data_count)
    grad_down, grad_up = finish(
        factor, place, quarter, first, second, first_peer, second_peer
    )
    return (grad_down, grad_up.reshape(2, RANK, SHARD))


def solution(mesh):
    in_specs = (
        P(("dp", "fsdp"), None),
        P(("dp", "fsdp")),
        P(("dp", "fsdp"), None),
        P(("dp", "fsdp"), None),
        P(("dp", "fsdp"), None),
        P(("dp", "fsdp"), None),
        P(None, "fsdp", None),
        P(None, None, "fsdp"),
    )
    out_specs = (P(None, "fsdp", None), P(None, None, "fsdp"))
    return jax.shard_map(local, mesh=mesh, in_specs=in_specs, out_specs=out_specs, check_vma=False)
```

```python
import functools
import math

import jax
import jax.numpy as jnp
from jax import lax
from jax.experimental import pallas as pl
from jax.experimental.pallas import tpu as pltpu
from jax.sharding import PartitionSpec as P

HEADS = 40
NSTEPS = 1000
AXES = ("dp", "fsdp")
NX, NY, NZ, NC = 4, 4, 8, 2
BF16 = jnp.bfloat16
F32 = jnp.float32
NORM_CHUNKS = 4
LOG2E = math.log2(math.e)

CLIP = 192
WIDTH = 5120
HALF = WIDTH // 2
SHARD = 640
RANK = 128
HEAD = 128
LOCAL_HEADS = SHARD // HEAD
VMEM_LIMIT = 24 * 1024 * 1024
SMALL = pl.CostEstimate(flops=1000, bytes_accessed=1000, transcendentals=0)


def linear(x, y, z, c):
    x, y, z, c = x % NX, y % NY, z % NZ, c % NC
    return (((x // 2) * NZ + z) * NC + c) * 8 + (x % 2) * NY + y


def permutation(target):
    pairs = []
    for x in range(NX):
        for y in range(NY):
            for z in range(NZ):
                for c in range(NC):
                    pairs.append((linear(x, y, z, c), linear(*target(x, y, z, c))))
    return pairs


def send(value, target):
    return lax.ppermute(value, AXES, permutation(target))


def swap_cores(value):
    return send(value, lambda x, y, z, c: (x, y, z, 1 - c))


def send_y(value, step):
    return send(value, lambda x, y, z, c: (x, y + step, z, c))


Z_GROUPS = [
    [linear(x, y, z, c) for z in range(NZ)]
    for x in range(NX)
    for y in range(NY)
    for c in range(NC)
]


def scatter_x(parts):
    return [
        parts[0],
        send(parts[1], lambda x, y, z, c: (x + 1, y, z, 1 - c)),
        send(parts[2], lambda x, y, z, c: (x + 2, y, z, c)),
        send(parts[3], lambda x, y, z, c: (x - 1, y, z, 1 - c)),
    ]


def scatter_y(parts):
    return [parts[0]] + [send_y(parts[step], step) for step in range(1, NY)]


def exchange_z(value):
    return lax.all_to_all(value, AXES, 0, 0, axis_index_groups=Z_GROUPS, tiled=True)


def dot(a, b, ca, cb):
    return lax.dot_general(a, b, (((ca,), (cb,)), ((), ())), preferred_element_type=F32)


def whole(shape):
    return pl.BlockSpec(shape, lambda *_: (0,) * len(shape))


SCALARS = pl.BlockSpec(memory_space=pltpu.SMEM)
RESIDENT = pl.BlockSpec(memory_space=pltpu.VMEM)
ANYWHERE = pl.BlockSpec(memory_space=pl.ANY)


def call(kernel, name, out_shape, scratch, place, resident, after=()):
    outs = [jax.ShapeDtypeStruct(shape, dtype) for shape, dtype in out_shape]
    return pl.pallas_call(
        kernel,
        out_shape=outs,
        in_specs=[SCALARS] + [RESIDENT] * len(resident) + [ANYWHERE] * len(after),
        out_specs=[RESIDENT] * len(outs),
        scratch_shapes=[pltpu.VMEM(shape, dtype) for shape, dtype in scratch],
        compiler_params=pltpu.CompilerParams(vmem_limit_bytes=VMEM_LIMIT),
        cost_estimate=SMALL,
        name=name,
    )(place, *resident, *after)


def normalize_kernel(place, states, q, k, v, g, nown, nsend, held, sems):
    mine = pl.multiple_of(place[0] * HALF, HALF)
    other = pl.multiple_of((1 - place[0]) * HALF, HALF)
    size = CLIP // NORM_CHUNKS
    chunks = [
        pltpu.make_async_copy(
            states.at[pl.ds(n * size, size)], held.at[pl.ds(n * size, size)], sems.at[n]
        )
        for n in range(NORM_CHUNKS)
    ]
    copies = [
        pltpu.make_async_copy(
            src.at[:, pl.ds(other, HALF)], nsend.at[n], sems.at[NORM_CHUNKS + n]
        )
        for n, src in enumerate((q, k, v, g))
    ]
    for copy in chunks + copies:
        copy.start()

    def block(step, carry):
        rows = pl.ds(pl.multiple_of(step * 16, 16), 16)
        inputs = held[rows, :].astype(F32)
        mean = jnp.mean(inputs, axis=1, keepdims=True)
        center = inputs - mean
        spread = jnp.mean(center * center, axis=1, keepdims=True)
        inverse = lax.rsqrt(spread + 1e-06)
        for begin, out in ((mine, nown), (other, nsend.at[4])):
            part = held[rows, pl.ds(begin, HALF)].astype(F32)
            out[rows, :] = ((part - mean) * inverse).astype(BF16)
        return carry

    for n, copy in enumerate(chunks):
        copy.wait()
        lax.fori_loop(n * size // 16, (n + 1) * size // 16, block, 0)
    for copy in copies:
        copy.wait()


def normalize(place, *arrays):
    return pl.pallas_call(
        normalize_kernel,
        out_shape=[
            jax.ShapeDtypeStruct((CLIP, HALF), BF16),
            jax.ShapeDtypeStruct((5, CLIP, HALF), BF16),
        ],
        in_specs=[SCALARS] + [pl.BlockSpec(memory_space=pl.ANY)] * 5,
        out_specs=[RESIDENT] * 2,
        scratch_shapes=[
            pltpu.VMEM((CLIP, WIDTH), BF16),
            pltpu.SemaphoreType.DMA((NORM_CHUNKS + 4,)),
        ],
        compiler_params=pltpu.CompilerParams(vmem_limit_bytes=VMEM_LIMIT),
        cost_estimate=SMALL,
        name="normalize",
    )(place, *(pltpu.with_memory_space_constraint(array, pltpu.HBM) for array in arrays))


def lower_kernel(place, nown, npeer, own, other, weight, out0, out1):
    core, y = place[2], place[1]
    total = jnp.zeros((2 * CLIP, 2 * RANK), F32)
    for step in range(NY):
        at = pl.ds(pl.multiple_of(lax.rem(y + step, NY) * SHARD, SHARD), SHARD)
        rows = jnp.concatenate([nown[:, at], npeer[4, :, at]], axis=0)
        total += dot(rows, jnp.concatenate([own[step], other[step]], axis=1), 1, 0)
    for clip, out in enumerate((out0, out1)):
        out[core, :CLIP] = total[clip * CLIP : (clip + 1) * CLIP, :RANK]
        out[1 - core, :CLIP] = total[clip * CLIP : (clip + 1) * CLIP, RANK:]
        out[0, CLIP:] = weight[...]
        out[1, CLIP:] = weight[...]


def lower(place, *arrays):
    return call(lower_kernel, "lower", [((2, CLIP + 8, RANK), F32)] * 2, [], place, arrays)


def attend_kernel(steps, first, after, place, *refs):
    count = len(steps)
    own, peer, lows, given = refs[:4], refs[4], refs[5:9], refs[9 : 9 + count]
    refs = refs[9 + count + after :]
    gups, dlow0, dlow1, rest = refs[:count], refs[count], refs[count + 1], refs[count + 2 :]
    if first:
        mine0, mine1, peer0, peer1 = lows
        low, weights, ups, dqs, dvs = rest
        for j in range(2):
            for clip in range(2):
                total = (mine0, mine1)[clip][j, :CLIP] + (peer1, peer0)[clip][j, :CLIP]
                low[j, clip * CLIP : (clip + 1) * CLIP] = total.astype(BF16)
        weights[0] = mine0[0, CLIP:]
        weights[1] = peer0[0, CLIP:]
    else:
        low, weights, in0, in1 = lows
        ups, dqs, dvs = rest
    core = place[2]
    scale = 1.0 / math.sqrt(HEAD)
    clips = [slice(clip * CLIP, (clip + 1) * CLIP) for clip in range(2)]

    def load(n, clip):
        shard = lax.rem(place[1] + steps[n], NY) * SHARD
        if clip == 0:
            at = pl.ds(pl.multiple_of(place[0] * HALF + shard, SHARD), SHARD)
            q, k, v, g = (r[:, at] for r in own)
        else:
            at = pl.ds(pl.multiple_of(shard, SHARD), SHARD)
            q, k, v, g = (peer[m, :, at] for m in range(4))
        rows = clips[clip]
        query = (q.astype(F32) + dot(low[0, rows], ups[n, 0], 1, 0)).astype(BF16)
        value = (v.astype(F32) + dot(low[1, rows], ups[n, 1], 1, 0)).astype(BF16)
        for h in range(LOCAL_HEADS):
            cols = slice(h * HEAD, (h + 1) * HEAD)
            heads.append((n, clip, cols, query[:, cols], k[:, cols], value[:, cols], g[:, cols]))

    def products(head):
        query, key, value, grad = head[3:]
        return dot(key, query, 1, 1), dot(value, grad, 1, 1)

    def finish(head, probs, dscores):
        n, clip, cols, query, key, value, grad = head
        weight = weights[clip, :1]
        dvs[n, clips[clip], cols] = (dot(probs, grad, 1, 0) * weight).astype(BF16)
        dqs[n, clips[clip], cols] = (dot(dscores, key, 0, 0) * (weight * scale)).astype(BF16)

    def collect(n):
        for j, grads in enumerate((dqs, dvs)):
            for clip, out in enumerate((dlow0, dlow1)):
                total = dot(grads[n, clips[clip]], ups[n, j], 1, 1)
                if n == 0:
                    out[j] = total if first else (in0, in1)[clip][j] + total
                else:
                    out[j] += total
            store_pieces(gups[n], j, dot(low[j], grads[n], 0, 0))

    heads = []
    for n in range(count):
        ups[n, core] = given[n][0]
        ups[n, 1 - core] = given[n][1]
        for clip in range(2):
            load(n, clip)

    ready = products(heads[0])
    done = None
    for at, head in enumerate(heads):
        scores, dprobs = ready
        if at + 1 < len(heads):
            ready = products(heads[at + 1])
        if done is not None:
            finish(*done)
            if head[0] != done[0][0]:
                collect(done[0][0])
        top = jnp.max(scores, axis=0, keepdims=True)
        powers = jnp.exp2((scores - top) * (scale * LOG2E))
        probs = powers * (1.0 / jnp.sum(powers, axis=0, keepdims=True))
        inner = jnp.sum(probs * dprobs, axis=0, keepdims=True)
        done = (head, probs.astype(BF16), (probs * (dprobs - inner)).astype(BF16))
    finish(*done)
    collect(count - 1)


def lane_blocks(rows):
    return jnp.concatenate(
        [rows[:, h * HEAD : (h + 1) * HEAD] for h in range(LOCAL_HEADS)], axis=0
    )


def store_pieces(out, j, total):
    for piece in range(RANK // 8):
        at = j * (RANK // 8) + piece
        out[at // NZ, at % NZ] = lane_blocks(total[piece * 8 : (piece + 1) * 8]).astype(BF16)


PIECES = (4, NZ, 40, 128)
LOWS = (2, CLIP, RANK)


def attend(steps, after, place, arrays, peer, ups, *lows):
    first, count = lows[0].dtype == F32, len(steps)
    shapes = [(PIECES, BF16)] * count + [(LOWS, F32)] * 2
    if first:
        shapes += [((2, 2 * CLIP, RANK), BF16), ((2, 8, RANK), F32)]
    scratch = [((count, 2, RANK, SHARD), BF16)] + [((count, 2 * CLIP, SHARD), BF16)] * 2
    kernel = functools.partial(attend_kernel, steps, first, len(after))
    given = [ups[step] for step in steps]
    return call(
        kernel, "attend", shapes, scratch, place, (*arrays, peer, *lows, *given), after
    )


def down_kernel(after, place, nown, peer, mine0, mine1, peer0, peer1, *refs):
    *outs, dlow, totals = refs[after:]
    for j in range(2):
        for clip in range(2):
            total = (mine0, mine1)[clip][j] + (peer1, peer0)[clip][j]
            dlow[j * RANK : (j + 1) * RANK, clip * CLIP : (clip + 1) * CLIP] = total.astype(BF16).T
    for shift in range(NY):
        shard = pl.multiple_of(lax.rem(place[1] + shift, NY) * SHARD, SHARD)
        normed = jnp.concatenate([nown[:, pl.ds(shard, SHARD)], peer[4, :, pl.ds(shard, SHARD)]], axis=0)
        totals[shift] = dot(dlow[...], normed, 1, 0)
        for step, out in enumerate(outs):
            first = lax.rem(place[3] + step, NX) * (2 * RANK // NX)
            for z in range(NZ):
                rows = totals[shift, pl.ds(pl.multiple_of(first + z * 8, 8), 8), :]
                out[shift, z] = lane_blocks(rows).astype(BF16)


def down_grads(place, nown, peer, dlows, *after):
    shapes = [((NY, *PIECES[1:]), BF16)] * NX
    scratch = [((2 * RANK, 2 * CLIP), BF16), ((NY, 2 * RANK, SHARD), F32)]
    kernel = functools.partial(down_kernel, len(after))
    return call(kernel, "down_grads", shapes, scratch, place, (nown, peer, *dlows), after)


def sum_y_kernel(place, *refs):
    parts, outs = refs[:4], refs[4:]
    x = place[3]
    for quarter in range(4):
        source = lax.rem(quarter + x, 4)
        for z in range(NZ):
            total = sum(r[source, z].astype(F32) for r in parts)
            outs[quarter][z] = total.astype(BF16)


def sum_y(place, parts):
    return pl.pallas_call(
        sum_y_kernel,
        out_shape=[jax.ShapeDtypeStruct(PIECES[1:], BF16)] * 4,
        in_specs=[pl.BlockSpec(memory_space=pltpu.SMEM)]
        + [pl.BlockSpec(memory_space=pltpu.VMEM)] * 4,
        out_specs=[pl.BlockSpec(memory_space=pltpu.VMEM)] * 4,
        compiler_params=pltpu.CompilerParams(vmem_limit_bytes=VMEM_LIMIT),
        cost_estimate=SMALL,
        name="sum_y",
    )(place, *parts)


def sum_x_kernel(*refs):
    parts, outs = refs[:4], refs[4:]
    for step in range(NY):
        outs[step][...] = sum(r[step].astype(F32) for r in parts).astype(BF16)


def sum_x(parts):
    return pl.pallas_call(
        sum_x_kernel,
        out_shape=[jax.ShapeDtypeStruct(PIECES[1:], BF16)] * NY,
        in_specs=[pl.BlockSpec(memory_space=pltpu.VMEM)] * 4,
        out_specs=[pl.BlockSpec(memory_space=pltpu.VMEM)] * NY,
        compiler_params=pltpu.CompilerParams(vmem_limit_bytes=VMEM_LIMIT),
        cost_estimate=SMALL,
        name="sum_x",
    )(*parts)


def join_kernel(*refs):
    ups, downs, out = refs[:4], refs[4:8], refs[8]
    for z in range(NZ):
        up = sum(r[z].astype(F32) for r in ups)
        down = sum(r[z].astype(F32) for r in downs)
        out[z] = jnp.concatenate([up, down], axis=0).astype(BF16)


def join(ups, downs):
    return pl.pallas_call(
        join_kernel,
        out_shape=jax.ShapeDtypeStruct((NZ, 80, 128), BF16),
        in_specs=[pl.BlockSpec(memory_space=pltpu.VMEM)] * 8,
        out_specs=pl.BlockSpec(memory_space=pltpu.VMEM),
        compiler_params=pltpu.CompilerParams(vmem_limit_bytes=VMEM_LIMIT),
        cost_estimate=SMALL,
        name="join",
    )(*ups, *downs)


def finish_kernel(factor, place, own, first, second, first_peer, second_peer, down, up, flat):
    core, x = place[2], place[3]

    def write(step, ref):
        quarter = lax.rem(x + step, 4)
        for z in range(NZ):
            part = ref[z].astype(F32) * factor
            for out, begin in ((up, 0), (flat, 40)):
                out[quarter * NZ + z] = jnp.concatenate(
                    [part[begin + h * 8 : begin + (h + 1) * 8] for h in range(LOCAL_HEADS)], axis=1
                )

    @pl.when(core == 0)
    def _():
        for step, ref in enumerate((own, second, first_peer, first)):
            write(step, ref)

    @pl.when(core == 1)
    def _():
        for step, ref in enumerate((second, second_peer, first, first_peer)):
            write(step, ref)

    for j in range(2):
        rows = flat[j * 2 * NZ : (j + 1) * 2 * NZ].reshape(RANK, SHARD)
        down[j] = rows.T


def finish(factor, place, *parts):
    return pl.pallas_call(
        functools.partial(finish_kernel, factor),
        out_shape=(
            jax.ShapeDtypeStruct((2, SHARD, RANK), F32),
            jax.ShapeDtypeStruct((4 * NZ, 8, SHARD), F32),
        ),
        in_specs=[pl.BlockSpec(memory_space=pltpu.SMEM)]
        + [pl.BlockSpec(memory_space=pltpu.VMEM)] * 5,
        out_specs=(pl.BlockSpec(memory_space=pltpu.VMEM),) * 2,
        scratch_shapes=[pltpu.VMEM((4 * NZ, 8, SHARD), F32)],
        compiler_params=pltpu.CompilerParams(vmem_limit_bytes=VMEM_LIMIT),
        name="finish",
    )(place, *parts)


def cross_x(part):
    other = send(part, lambda x, y, z, c: (x - 1, y, z, 1) if c == 0 else (x, y, z, 0))
    own = send(part, lambda x, y, z, c: (x, y, z, 0) if c == 0 else (x + 1, y, z, 1))
    return own, other


def local(states, steps, q, k, v, g, down_maps, up_maps):
    dp, fsdp = lax.axis_index("dp"), lax.axis_index("fsdp")
    core, x_lo, y = dp % 2, fsdp // NY, fsdp % NY
    x = (dp // (2 * NZ)) * 2 + x_lo
    place = jnp.stack([x_lo ^ core, y, core, x]).astype(jnp.int32)
    weight = (steps[0].astype(F32) + 1.0) / NSTEPS
    weight = jnp.full((8, RANK), weight, F32)

    down_part = lax.dynamic_index_in_dim(down_maps, core, 0, keepdims=False)
    up_part = lax.dynamic_index_in_dim(up_maps, core, 0, keepdims=False)
    nown, nsend = normalize(place, states, q, k, v, g)
    downs = [send_y(down_part, -step) for step in range(1, NY)]
    up = jnp.stack(cross_x(up_part))
    nsend, up, *downs = lax.optimization_barrier((nsend, up, *downs))
    downs = cross_x(jnp.stack([down_part, *downs]))
    ups = [up] + [send_y(up, -step) for step in range(1, NY)]
    peer = swap_cores(nsend)

    lows = lower(place, nown, peer, *downs, weight)
    lows = [*lows, *(swap_cores(part) for part in lows)]
    rows = (place, (q, k, v, g), peer, ups)
    gups = [None] * NY
    gups[1], gups[3], gups[0], *dlow, low, weights = attend((1, 3, 0), (), *rows, *lows)
    gups[1], gups[3] = send_y(gups[1], 1), send_y(gups[3], 3)
    gups[2], *dlow = attend((2,), (), *rows, low, weights, *dlow)
    gups[2] = send_y(gups[2], 2)
    dlows = [*dlow, *(swap_cores(part) for part in dlow)]
    gdowns = scatter_x(down_grads(place, nown, peer, dlows))
    ups = scatter_x(sum_y(place, gups))
    downs = scatter_y(sum_x(gdowns))
    eighths = join(ups, downs)
    eighths = exchange_z(eighths)
    piece = jnp.sum(eighths.astype(F32), axis=0).astype(BF16)
    quarter = exchange_z(jnp.broadcast_to(piece, (NZ, 80, 128)))

    first = send(
        quarter, lambda x, y, z, c: (x + 2, y, z, 1) if c == 0 else (x + 1, y, z, 0)
    )
    second = send(
        quarter, lambda x, y, z, c: (x, y, z, 1) if c == 0 else (x - 1, y, z, 0)
    )
    first_peer = swap_cores(first)
    second_peer = swap_cores(second)
    data_count = lax.axis_size("dp") * lax.axis_size("fsdp")
    factor = 1.0 / math.sqrt(CLIP * data_count)
    grad_down, grad_up = finish(
        factor, place, quarter, first, second, first_peer, second_peer
    )
    return (grad_down, grad_up.reshape(2, RANK, SHARD))


def solution(mesh):
    in_specs = (
        P(("dp", "fsdp"), None),
        P(("dp", "fsdp")),
        P(("dp", "fsdp"), None),
        P(("dp", "fsdp"), None),
        P(("dp", "fsdp"), None),
        P(("dp", "fsdp"), None),
        P(None, "fsdp", None),
        P(None, None, "fsdp"),
    )
    out_specs = (P(None, "fsdp", None), P(None, None, "fsdp"))
    return jax.shard_map(local, mesh=mesh, in_specs=in_specs, out_specs=out_specs, check_vma=False)
```

```python
import functools
import math

import jax
import jax.numpy as jnp
from jax import lax
from jax.experimental import pallas as pl
from jax.experimental.pallas import tpu as pltpu
from jax.sharding import PartitionSpec as P

HEADS = 40
NSTEPS = 1000
AXES = ("dp", "fsdp")
NX, NY, NZ, NC = 4, 4, 8, 2
BF16 = jnp.bfloat16
F32 = jnp.float32
NORM_CHUNKS = 4
LOG2E = math.log2(math.e)

CLIP = 192
WIDTH = 5120
HALF = WIDTH // 2
SHARD = 640
RANK = 128
HEAD = 128
LOCAL_HEADS = SHARD // HEAD
VMEM_LIMIT = 24 * 1024 * 1024
SMALL = pl.CostEstimate(flops=1000, bytes_accessed=1000, transcendentals=0)


def linear(x, y, z, c):
    x, y, z, c = x % NX, y % NY, z % NZ, c % NC
    return (((x // 2) * NZ + z) * NC + c) * 8 + (x % 2) * NY + y


def permutation(target):
    pairs = []
    for x in range(NX):
        for y in range(NY):
            for z in range(NZ):
                for c in range(NC):
                    pairs.append((linear(x, y, z, c), linear(*target(x, y, z, c))))
    return pairs


def send(value, target):
    return lax.ppermute(value, AXES, permutation(target))


def swap_cores(value):
    return send(value, lambda x, y, z, c: (x, y, z, 1 - c))


def send_y(value, step):
    return send(value, lambda x, y, z, c: (x, y + step, z, c))


Z_GROUPS = [
    [linear(x, y, z, c) for z in range(NZ)]
    for x in range(NX)
    for y in range(NY)
    for c in range(NC)
]


def scatter_x(parts):
    across = send(parts[2], lambda x, y, z, c: (x + 2, y, z, c))
    after = send(parts[1], lambda x, y, z, c: (x + 1, y, z, 1 - c))
    before = send(parts[3], lambda x, y, z, c: (x - 1, y, z, 1 - c))
    return [parts[0], across, after, before]


def scatter_y(parts):
    across = send_y(parts[2], 2)
    return [parts[0], across, send_y(parts[1], 1), send_y(parts[3], 3)]


def exchange_z(value):
    return lax.all_to_all(value, AXES, 0, 0, axis_index_groups=Z_GROUPS, tiled=True)


def dot(a, b, ca, cb):
    return lax.dot_general(a, b, (((ca,), (cb,)), ((), ())), preferred_element_type=F32)


def whole(shape):
    return pl.BlockSpec(shape, lambda *_: (0,) * len(shape))


SCALARS = pl.BlockSpec(memory_space=pltpu.SMEM)
RESIDENT = pl.BlockSpec(memory_space=pltpu.VMEM)
ANYWHERE = pl.BlockSpec(memory_space=pl.ANY)


def call(kernel, name, out_shape, scratch, place, resident, after=()):
    outs = [jax.ShapeDtypeStruct(shape, dtype) for shape, dtype in out_shape]
    return pl.pallas_call(
        kernel,
        out_shape=outs,
        in_specs=[SCALARS] + [RESIDENT] * len(resident) + [ANYWHERE] * len(after),
        out_specs=[RESIDENT] * len(outs),
        scratch_shapes=[pltpu.VMEM(shape, dtype) for shape, dtype in scratch],
        compiler_params=pltpu.CompilerParams(vmem_limit_bytes=VMEM_LIMIT),
        cost_estimate=SMALL,
        name=name,
    )(place, *resident, *after)


def normalize_kernel(place, states, q, k, v, g, nown, nsend, held, sems):
    mine = pl.multiple_of(place[0] * HALF, HALF)
    other = pl.multiple_of((1 - place[0]) * HALF, HALF)
    size = CLIP // NORM_CHUNKS
    chunks = [
        pltpu.make_async_copy(
            states.at[pl.ds(n * size, size)], held.at[pl.ds(n * size, size)], sems.at[n]
        )
        for n in range(NORM_CHUNKS)
    ]
    copies = [
        pltpu.make_async_copy(
            src.at[:, pl.ds(other, HALF)], nsend.at[n], sems.at[NORM_CHUNKS + n]
        )
        for n, src in enumerate((q, k, v, g))
    ]
    for copy in chunks + copies:
        copy.start()

    def block(step, carry):
        rows = pl.ds(pl.multiple_of(step * 16, 16), 16)
        inputs = held[rows, :].astype(F32)
        mean = jnp.mean(inputs, axis=1, keepdims=True)
        center = inputs - mean
        spread = jnp.mean(center * center, axis=1, keepdims=True)
        inverse = lax.rsqrt(spread + 1e-06)
        for begin, out in ((mine, nown), (other, nsend.at[4])):
            part = held[rows, pl.ds(begin, HALF)].astype(F32)
            out[rows, :] = ((part - mean) * inverse).astype(BF16)
        return carry

    for n, copy in enumerate(chunks):
        copy.wait()
        lax.fori_loop(n * size // 16, (n + 1) * size // 16, block, 0)
    for copy in copies:
        copy.wait()


def normalize(place, *arrays):
    return pl.pallas_call(
        normalize_kernel,
        out_shape=[
            jax.ShapeDtypeStruct((CLIP, HALF), BF16),
            jax.ShapeDtypeStruct((5, CLIP, HALF), BF16),
        ],
        in_specs=[SCALARS] + [pl.BlockSpec(memory_space=pl.ANY)] * 5,
        out_specs=[RESIDENT] * 2,
        scratch_shapes=[
            pltpu.VMEM((CLIP, WIDTH), BF16),
            pltpu.SemaphoreType.DMA((NORM_CHUNKS + 4,)),
        ],
        compiler_params=pltpu.CompilerParams(vmem_limit_bytes=VMEM_LIMIT),
        cost_estimate=SMALL,
        name="normalize",
    )(place, *(pltpu.with_memory_space_constraint(array, pltpu.HBM) for array in arrays))


def lower_kernel(place, nown, npeer, own, other, weight, out0, out1):
    core, y = place[2], place[1]
    total = jnp.zeros((2 * CLIP, 2 * RANK), F32)
    for step in range(NY):
        at = pl.ds(pl.multiple_of(lax.rem(y + step, NY) * SHARD, SHARD), SHARD)
        rows = jnp.concatenate([nown[:, at], npeer[4, :, at]], axis=0)
        total += dot(rows, jnp.concatenate([own[step], other[step]], axis=1), 1, 0)
    for clip, out in enumerate((out0, out1)):
        out[core, :CLIP] = total[clip * CLIP : (clip + 1) * CLIP, :RANK]
        out[1 - core, :CLIP] = total[clip * CLIP : (clip + 1) * CLIP, RANK:]
        out[0, CLIP:] = weight[...]
        out[1, CLIP:] = weight[...]


def lower(place, *arrays):
    return call(lower_kernel, "lower", [((2, CLIP + 8, RANK), F32)] * 2, [], place, arrays)


def attend_kernel(steps, first, after, place, *refs):
    count = len(steps)
    own, peer, lows, given = refs[:4], refs[4], refs[5:9], refs[9 : 9 + count]
    refs = refs[9 + count + after :]
    gups, dlow0, dlow1, rest = refs[:count], refs[count], refs[count + 1], refs[count + 2 :]
    if first:
        mine0, mine1, peer0, peer1 = lows
        low, weights, ups, dqs, dvs = rest
        for j in range(2):
            for clip in range(2):
                total = (mine0, mine1)[clip][j, :CLIP] + (peer1, peer0)[clip][j, :CLIP]
                low[j, clip * CLIP : (clip + 1) * CLIP] = total.astype(BF16)
        weights[0] = mine0[0, CLIP:]
        weights[1] = peer0[0, CLIP:]
    else:
        low, weights, in0, in1 = lows
        ups, dqs, dvs = rest
    core = place[2]
    scale = 1.0 / math.sqrt(HEAD)
    clips = [slice(clip * CLIP, (clip + 1) * CLIP) for clip in range(2)]

    def load(n, clip):
        shard = lax.rem(place[1] + steps[n], NY) * SHARD
        if clip == 0:
            at = pl.ds(pl.multiple_of(place[0] * HALF + shard, SHARD), SHARD)
            q, k, v, g = (r[:, at] for r in own)
        else:
            at = pl.ds(pl.multiple_of(shard, SHARD), SHARD)
            q, k, v, g = (peer[m, :, at] for m in range(4))
        rows = clips[clip]
        query = (q.astype(F32) + dot(low[0, rows], ups[n, 0], 1, 0)).astype(BF16)
        value = (v.astype(F32) + dot(low[1, rows], ups[n, 1], 1, 0)).astype(BF16)
        for h in range(LOCAL_HEADS):
            cols = slice(h * HEAD, (h + 1) * HEAD)
            heads.append((n, clip, cols, query[:, cols], k[:, cols], value[:, cols], g[:, cols]))

    def products(head):
        query, key, value, grad = head[3:]
        return dot(key, query, 1, 1), dot(value, grad, 1, 1)

    def finish(head, probs, dscores):
        n, clip, cols, query, key, value, grad = head
        weight = weights[clip, :1]
        dvs[n, clips[clip], cols] = (dot(probs, grad, 1, 0) * weight).astype(BF16)
        dqs[n, clips[clip], cols] = (dot(dscores, key, 0, 0) * (weight * scale)).astype(BF16)

    def collect(n):
        for j, grads in enumerate((dqs, dvs)):
            for clip, out in enumerate((dlow0, dlow1)):
                total = dot(grads[n, clips[clip]], ups[n, j], 1, 1)
                if n == 0:
                    out[j] = total if first else (in0, in1)[clip][j] + total
                else:
                    out[j] += total
            store_pieces(gups[n], j, dot(low[j], grads[n], 0, 0))

    heads = []
    for n in range(count):
        ups[n, core] = given[n][0]
        ups[n, 1 - core] = given[n][1]
        for clip in range(2):
            load(n, clip)

    ready = products(heads[0])
    done = None
    for at, head in enumerate(heads):
        scores, dprobs = ready
        if at + 1 < len(heads):
            ready = products(heads[at + 1])
        if done is not None:
            finish(*done)
            if head[0] != done[0][0]:
                collect(done[0][0])
        top = jnp.max(scores, axis=0, keepdims=True)
        powers = jnp.exp2((scores - top) * (scale * LOG2E))
        probs = powers * (1.0 / jnp.sum(powers, axis=0, keepdims=True))
        inner = jnp.sum(probs * dprobs, axis=0, keepdims=True)
        done = (head, probs.astype(BF16), (probs * (dprobs - inner)).astype(BF16))
    finish(*done)
    collect(count - 1)


def lane_blocks(rows):
    return jnp.concatenate(
        [rows[:, h * HEAD : (h + 1) * HEAD] for h in range(LOCAL_HEADS)], axis=0
    )


def store_pieces(out, j, total):
    for piece in range(RANK // 8):
        at = j * (RANK // 8) + piece
        out[at // NZ, at % NZ] = lane_blocks(total[piece * 8 : (piece + 1) * 8]).astype(BF16)


PIECES = (4, NZ, 40, 128)
LOWS = (2, CLIP, RANK)


def attend(steps, after, place, arrays, peer, ups, *lows):
    first, count = lows[0].dtype == F32, len(steps)
    shapes = [(PIECES, BF16)] * count + [(LOWS, F32)] * 2
    if first:
        shapes += [((2, 2 * CLIP, RANK), BF16), ((2, 8, RANK), F32)]
    scratch = [((count, 2, RANK, SHARD), BF16)] + [((count, 2 * CLIP, SHARD), BF16)] * 2
    kernel = functools.partial(attend_kernel, steps, first, len(after))
    given = [ups[step] for step in steps]
    return call(
        kernel, "attend", shapes, scratch, place, (*arrays, peer, *lows, *given), after
    )


def down_kernel(after, place, nown, peer, mine0, mine1, peer0, peer1, *refs):
    *outs, dlow, totals = refs[after:]
    for j in range(2):
        for clip in range(2):
            total = (mine0, mine1)[clip][j] + (peer1, peer0)[clip][j]
            dlow[j * RANK : (j + 1) * RANK, clip * CLIP : (clip + 1) * CLIP] = total.astype(BF16).T
    for shift in range(NY):
        shard = pl.multiple_of(lax.rem(place[1] + shift, NY) * SHARD, SHARD)
        normed = jnp.concatenate([nown[:, pl.ds(shard, SHARD)], peer[4, :, pl.ds(shard, SHARD)]], axis=0)
        totals[shift] = dot(dlow[...], normed, 1, 0)
        for step, out in enumerate(outs):
            first = lax.rem(place[3] + step, NX) * (2 * RANK // NX)
            for z in range(NZ):
                rows = totals[shift, pl.ds(pl.multiple_of(first + z * 8, 8), 8), :]
                out[shift, z] = lane_blocks(rows).astype(BF16)


def down_grads(place, nown, peer, dlows, *after):
    shapes = [((NY, *PIECES[1:]), BF16)] * NX
    scratch = [((2 * RANK, 2 * CLIP), BF16), ((NY, 2 * RANK, SHARD), F32)]
    kernel = functools.partial(down_kernel, len(after))
    return call(kernel, "down_grads", shapes, scratch, place, (nown, peer, *dlows), after)


def sum_y_kernel(place, *refs):
    parts, outs = refs[:4], refs[4:]
    x = place[3]
    for quarter in range(4):
        source = lax.rem(quarter + x, 4)
        for z in range(NZ):
            total = sum(r[source, z].astype(F32) for r in parts)
            outs[quarter][z] = total.astype(BF16)


def sum_y(place, parts):
    return pl.pallas_call(
        sum_y_kernel,
        out_shape=[jax.ShapeDtypeStruct(PIECES[1:], BF16)] * 4,
        in_specs=[pl.BlockSpec(memory_space=pltpu.SMEM)]
        + [pl.BlockSpec(memory_space=pltpu.VMEM)] * 4,
        out_specs=[pl.BlockSpec(memory_space=pltpu.VMEM)] * 4,
        compiler_params=pltpu.CompilerParams(vmem_limit_bytes=VMEM_LIMIT),
        cost_estimate=SMALL,
        name="sum_y",
    )(place, *parts)


def sum_x_kernel(*refs):
    parts, outs = refs[:4], refs[4:]
    for step in range(NY):
        outs[step][...] = sum(r[step].astype(F32) for r in parts).astype(BF16)


def sum_x(parts):
    return pl.pallas_call(
        sum_x_kernel,
        out_shape=[jax.ShapeDtypeStruct(PIECES[1:], BF16)] * NY,
        in_specs=[pl.BlockSpec(memory_space=pltpu.VMEM)] * 4,
        out_specs=[pl.BlockSpec(memory_space=pltpu.VMEM)] * NY,
        compiler_params=pltpu.CompilerParams(vmem_limit_bytes=VMEM_LIMIT),
        cost_estimate=SMALL,
        name="sum_x",
    )(*parts)


def join_kernel(*refs):
    ups, downs, out = refs[:4], refs[4:8], refs[8]
    for z in range(NZ):
        up = sum(r[z].astype(F32) for r in ups)
        down = sum(r[z].astype(F32) for r in downs)
        out[z] = jnp.concatenate([up, down], axis=0).astype(BF16)


def join(ups, downs):
    return pl.pallas_call(
        join_kernel,
        out_shape=jax.ShapeDtypeStruct((NZ, 80, 128), BF16),
        in_specs=[pl.BlockSpec(memory_space=pltpu.VMEM)] * 8,
        out_specs=pl.BlockSpec(memory_space=pltpu.VMEM),
        compiler_params=pltpu.CompilerParams(vmem_limit_bytes=VMEM_LIMIT),
        cost_estimate=SMALL,
        name="join",
    )(*ups, *downs)


def finish_kernel(factor, place, own, first, second, first_peer, second_peer, down, up, flat):
    core, x = place[2], place[3]

    def write(step, ref):
        quarter = lax.rem(x + step, 4)
        for z in range(NZ):
            part = ref[z].astype(F32) * factor
            for out, begin in ((up, 0), (flat, 40)):
                out[quarter * NZ + z] = jnp.concatenate(
                    [part[begin + h * 8 : begin + (h + 1) * 8] for h in range(LOCAL_HEADS)], axis=1
                )

    @pl.when(core == 0)
    def _():
        for step, ref in enumerate((own, second, first_peer, first)):
            write(step, ref)

    @pl.when(core == 1)
    def _():
        for step, ref in enumerate((second, second_peer, first, first_peer)):
            write(step, ref)

    for j in range(2):
        rows = flat[j * 2 * NZ : (j + 1) * 2 * NZ].reshape(RANK, SHARD)
        down[j] = rows.T


def finish(factor, place, *parts):
    return pl.pallas_call(
        functools.partial(finish_kernel, factor),
        out_shape=(
            jax.ShapeDtypeStruct((2, SHARD, RANK), F32),
            jax.ShapeDtypeStruct((4 * NZ, 8, SHARD), F32),
        ),
        in_specs=[pl.BlockSpec(memory_space=pltpu.SMEM)]
        + [pl.BlockSpec(memory_space=pltpu.VMEM)] * 5,
        out_specs=(pl.BlockSpec(memory_space=pltpu.VMEM),) * 2,
        scratch_shapes=[pltpu.VMEM((4 * NZ, 8, SHARD), F32)],
        compiler_params=pltpu.CompilerParams(vmem_limit_bytes=VMEM_LIMIT),
        name="finish",
    )(place, *parts)


def cross_x(part):
    other = send(part, lambda x, y, z, c: (x - 1, y, z, 1) if c == 0 else (x, y, z, 0))
    own = send(part, lambda x, y, z, c: (x, y, z, 0) if c == 0 else (x + 1, y, z, 1))
    return own, other


def local(states, steps, q, k, v, g, down_maps, up_maps):
    dp, fsdp = lax.axis_index("dp"), lax.axis_index("fsdp")
    core, x_lo, y = dp % 2, fsdp // NY, fsdp % NY
    x = (dp // (2 * NZ)) * 2 + x_lo
    place = jnp.stack([x_lo ^ core, y, core, x]).astype(jnp.int32)
    weight = (steps[0].astype(F32) + 1.0) / NSTEPS
    weight = jnp.full((8, RANK), weight, F32)

    down_part = lax.dynamic_index_in_dim(down_maps, core, 0, keepdims=False)
    up_part = lax.dynamic_index_in_dim(up_maps, core, 0, keepdims=False)
    nown, nsend = normalize(place, states, q, k, v, g)
    downs = [send_y(down_part, -step) for step in range(1, NY)]
    up = jnp.stack(cross_x(up_part))
    nsend, up, *downs = lax.optimization_barrier((nsend, up, *downs))
    downs = cross_x(jnp.stack([down_part, *downs]))
    ups = [up] + [send_y(up, -step) for step in range(1, NY)]
    peer = swap_cores(nsend)

    lows = lower(place, nown, peer, *downs, weight)
    lows = [*lows, *(swap_cores(part) for part in lows)]
    rows = (place, (q, k, v, g), peer, ups)
    gups = [None] * NY
    gups[1], gups[3], gups[0], *dlow, low, weights = attend((1, 3, 0), (), *rows, *lows)
    gups[1], gups[3] = send_y(gups[1], 1), send_y(gups[3], 3)
    gups[2], *dlow = attend((2,), (), *rows, low, weights, *dlow)
    gups[2] = send_y(gups[2], 2)
    dlows = [*dlow, *(swap_cores(part) for part in dlow)]
    gdowns = scatter_x(down_grads(place, nown, peer, dlows))
    ups = scatter_x(sum_y(place, gups))
    downs = scatter_y(sum_x(gdowns))
    eighths = join(ups, downs)
    eighths = exchange_z(eighths)
    piece = jnp.sum(eighths.astype(F32), axis=0).astype(BF16)
    quarter = exchange_z(jnp.broadcast_to(piece, (NZ, 80, 128)))

    first = send(
        quarter, lambda x, y, z, c: (x + 2, y, z, 1) if c == 0 else (x + 1, y, z, 0)
    )
    second = send(
        quarter, lambda x, y, z, c: (x, y, z, 1) if c == 0 else (x - 1, y, z, 0)
    )
    first_peer = swap_cores(first)
    second_peer = swap_cores(second)
    data_count = lax.axis_size("dp") * lax.axis_size("fsdp")
    factor = 1.0 / math.sqrt(CLIP * data_count)
    grad_down, grad_up = finish(
        factor, place, quarter, first, second, first_peer, second_peer
    )
    return (grad_down, grad_up.reshape(2, RANK, SHARD))


def solution(mesh):
    in_specs = (
        P(("dp", "fsdp"), None),
        P(("dp", "fsdp")),
        P(("dp", "fsdp"), None),
        P(("dp", "fsdp"), None),
        P(("dp", "fsdp"), None),
        P(("dp", "fsdp"), None),
        P(None, "fsdp", None),
        P(None, None, "fsdp"),
    )
    out_specs = (P(None, "fsdp", None), P(None, None, "fsdp"))
    return jax.shard_map(local, mesh=mesh, in_specs=in_specs, out_specs=out_specs, check_vma=False)
```

```python
import functools
import math

import jax
import jax.numpy as jnp
from jax import lax
from jax.experimental import pallas as pl
from jax.experimental.pallas import tpu as pltpu
from jax.sharding import PartitionSpec as P

HEADS = 40
NSTEPS = 1000
AXES = ("dp", "fsdp")
NX, NY, NZ, NC = 4, 4, 8, 2
BF16 = jnp.bfloat16
F32 = jnp.float32
NORM_CHUNKS = 4
LOG2E = math.log2(math.e)

CLIP = 192
WIDTH = 5120
HALF = WIDTH // 2
SHARD = 640
RANK = 128
HEAD = 128
LOCAL_HEADS = SHARD // HEAD
VMEM_LIMIT = 24 * 1024 * 1024
SMALL = pl.CostEstimate(flops=1000, bytes_accessed=1000, transcendentals=0)


def linear(x, y, z, c):
    x, y, z, c = x % NX, y % NY, z % NZ, c % NC
    return (((x // 2) * NZ + z) * NC + c) * 8 + (x % 2) * NY + y


def permutation(target):
    pairs = []
    for x in range(NX):
        for y in range(NY):
            for z in range(NZ):
                for c in range(NC):
                    pairs.append((linear(x, y, z, c), linear(*target(x, y, z, c))))
    return pairs


def send(value, target):
    return lax.ppermute(value, AXES, permutation(target))


def swap_cores(value):
    return send(value, lambda x, y, z, c: (x, y, z, 1 - c))


def send_y(value, step):
    return send(value, lambda x, y, z, c: (x, y + step, z, c))


Z_GROUPS = [
    [linear(x, y, z, c) for z in range(NZ)]
    for x in range(NX)
    for y in range(NY)
    for c in range(NC)
]


def scatter_x(parts):
    across = send(parts[2], lambda x, y, z, c: (x + 2, y, z, c))
    after = send(parts[1], lambda x, y, z, c: (x + 1, y, z, 1 - c))
    before = send(parts[3], lambda x, y, z, c: (x - 1, y, z, 1 - c))
    return [parts[0], across, after, before]


def scatter_y(parts):
    across = send_y(parts[2], 2)
    return [parts[0], across, send_y(parts[1], 1), send_y(parts[3], 3)]


def exchange_z(value):
    return lax.all_to_all(value, AXES, 0, 0, axis_index_groups=Z_GROUPS, tiled=True)


def dot(a, b, ca, cb):
    return lax.dot_general(a, b, (((ca,), (cb,)), ((), ())), preferred_element_type=F32)


def whole(shape):
    return pl.BlockSpec(shape, lambda *_: (0,) * len(shape))


SCALARS = pl.BlockSpec(memory_space=pltpu.SMEM)
RESIDENT = pl.BlockSpec(memory_space=pltpu.VMEM)
ANYWHERE = pl.BlockSpec(memory_space=pl.ANY)


def call(kernel, name, out_shape, scratch, place, resident, after=()):
    outs = [jax.ShapeDtypeStruct(shape, dtype) for shape, dtype in out_shape]
    return pl.pallas_call(
        kernel,
        out_shape=outs,
        in_specs=[SCALARS] + [RESIDENT] * len(resident) + [ANYWHERE] * len(after),
        out_specs=[RESIDENT] * len(outs),
        scratch_shapes=[pltpu.VMEM(shape, dtype) for shape, dtype in scratch],
        compiler_params=pltpu.CompilerParams(vmem_limit_bytes=VMEM_LIMIT),
        cost_estimate=SMALL,
        name=name,
    )(place, *resident, *after)


def normalize_kernel(place, states, q, k, v, g, nown, nsend, held, sems):
    mine = pl.multiple_of(place[0] * HALF, HALF)
    other = pl.multiple_of((1 - place[0]) * HALF, HALF)
    size = CLIP // NORM_CHUNKS
    chunks = [
        pltpu.make_async_copy(
            states.at[pl.ds(n * size, size)], held.at[pl.ds(n * size, size)], sems.at[n]
        )
        for n in range(NORM_CHUNKS)
    ]
    copies = [
        pltpu.make_async_copy(
            src.at[:, pl.ds(other, HALF)], nsend.at[n], sems.at[NORM_CHUNKS + n]
        )
        for n, src in enumerate((q, k, v, g))
    ]
    for copy in chunks + copies:
        copy.start()

    def block(step, carry):
        rows = pl.ds(pl.multiple_of(step * 16, 16), 16)
        inputs = held[rows, :].astype(F32)
        mean = jnp.mean(inputs, axis=1, keepdims=True)
        center = inputs - mean
        spread = jnp.mean(center * center, axis=1, keepdims=True)
        inverse = lax.rsqrt(spread + 1e-06)
        for begin, out in ((mine, nown), (other, nsend.at[4])):
            part = held[rows, pl.ds(begin, HALF)].astype(F32)
            out[rows, :] = ((part - mean) * inverse).astype(BF16)
        return carry

    for n, copy in enumerate(chunks):
        copy.wait()
        lax.fori_loop(n * size // 16, (n + 1) * size // 16, block, 0)
    for copy in copies:
        copy.wait()


def normalize(place, *arrays):
    return pl.pallas_call(
        normalize_kernel,
        out_shape=[
            jax.ShapeDtypeStruct((CLIP, HALF), BF16),
            jax.ShapeDtypeStruct((5, CLIP, HALF), BF16),
        ],
        in_specs=[SCALARS] + [pl.BlockSpec(memory_space=pl.ANY)] * 5,
        out_specs=[RESIDENT] * 2,
        scratch_shapes=[
            pltpu.VMEM((CLIP, WIDTH), BF16),
            pltpu.SemaphoreType.DMA((NORM_CHUNKS + 4,)),
        ],
        compiler_params=pltpu.CompilerParams(vmem_limit_bytes=VMEM_LIMIT),
        cost_estimate=SMALL,
        name="normalize",
    )(place, *(pltpu.with_memory_space_constraint(array, pltpu.HBM) for array in arrays))


def lower_kernel(place, nown, npeer, own, other, weight, out0, out1):
    core, y = place[2], place[1]
    total = jnp.zeros((2 * CLIP, 2 * RANK), F32)
    for step in range(NY):
        at = pl.ds(pl.multiple_of(lax.rem(y + step, NY) * SHARD, SHARD), SHARD)
        rows = jnp.concatenate([nown[:, at], npeer[4, :, at]], axis=0)
        total += dot(rows, jnp.concatenate([own[step], other[step]], axis=1), 1, 0)
    for clip, out in enumerate((out0, out1)):
        out[core, :CLIP] = total[clip * CLIP : (clip + 1) * CLIP, :RANK]
        out[1 - core, :CLIP] = total[clip * CLIP : (clip + 1) * CLIP, RANK:]
        out[0, CLIP:] = weight[...]
        out[1, CLIP:] = weight[...]


def lower(place, *arrays):
    return call(lower_kernel, "lower", [((2, CLIP + 8, RANK), F32)] * 2, [], place, arrays)


def attend_kernel(steps, first, after, place, *refs):
    count = len(steps)
    own, peer, lows, given = refs[:4], refs[4], refs[5:9], refs[9 : 9 + count]
    refs = refs[9 + count + after :]
    gups, dlow0, dlow1, rest = refs[:count], refs[count], refs[count + 1], refs[count + 2 :]
    if first:
        mine0, mine1, peer0, peer1 = lows
        low, weights, ups, dqs, dvs = rest
        for j in range(2):
            for clip in range(2):
                total = (mine0, mine1)[clip][j, :CLIP] + (peer1, peer0)[clip][j, :CLIP]
                low[j, clip * CLIP : (clip + 1) * CLIP] = total.astype(BF16)
        weights[0] = mine0[0, CLIP:]
        weights[1] = peer0[0, CLIP:]
    else:
        low, weights, in0, in1 = lows
        ups, dqs, dvs = rest
    core = place[2]
    scale = 1.0 / math.sqrt(HEAD)
    clips = [slice(clip * CLIP, (clip + 1) * CLIP) for clip in range(2)]

    def load(n, clip):
        shard = lax.rem(place[1] + steps[n], NY) * SHARD
        if clip == 0:
            at = pl.ds(pl.multiple_of(place[0] * HALF + shard, SHARD), SHARD)
            q, k, v, g = (r[:, at] for r in own)
        else:
            at = pl.ds(pl.multiple_of(shard, SHARD), SHARD)
            q, k, v, g = (peer[m, :, at] for m in range(4))
        rows = clips[clip]
        query = (q.astype(F32) + dot(low[0, rows], ups[n, 0], 1, 0)).astype(BF16)
        value = (v.astype(F32) + dot(low[1, rows], ups[n, 1], 1, 0)).astype(BF16)
        for h in range(LOCAL_HEADS):
            cols = slice(h * HEAD, (h + 1) * HEAD)
            heads.append((n, clip, cols, query[:, cols], k[:, cols], value[:, cols], g[:, cols]))

    def products(head):
        query, key, value, grad = head[3:]
        return dot(key, query, 1, 1), dot(value, grad, 1, 1)

    def finish(head, probs, dscores):
        n, clip, cols, query, key, value, grad = head
        weight = weights[clip, :1]
        dvs[n, clips[clip], cols] = (dot(probs, grad, 1, 0) * weight).astype(BF16)
        dqs[n, clips[clip], cols] = (dot(dscores, key, 0, 0) * (weight * scale)).astype(BF16)

    def collect(n):
        for j, grads in enumerate((dqs, dvs)):
            for clip, out in enumerate((dlow0, dlow1)):
                total = dot(grads[n, clips[clip]], ups[n, j], 1, 1)
                if n == 0:
                    out[j] = total if first else (in0, in1)[clip][j] + total
                else:
                    out[j] += total
            store_pieces(gups[n], j, dot(low[j], grads[n], 0, 0))

    heads = []
    for n in range(count):
        ups[n, core] = given[n][0]
        ups[n, 1 - core] = given[n][1]
        for clip in range(2):
            load(n, clip)

    ready = products(heads[0])
    done = None
    for at, head in enumerate(heads):
        scores, dprobs = ready
        if at + 1 < len(heads):
            ready = products(heads[at + 1])
        if done is not None:
            finish(*done)
            if head[0] != done[0][0]:
                collect(done[0][0])
        top = jnp.max(scores, axis=0, keepdims=True)
        powers = jnp.exp2((scores - top) * (scale * LOG2E))
        probs = powers * (1.0 / jnp.sum(powers, axis=0, keepdims=True))
        inner = jnp.sum(probs * dprobs, axis=0, keepdims=True)
        done = (head, probs.astype(BF16), (probs * (dprobs - inner)).astype(BF16))
    finish(*done)
    collect(count - 1)


def lane_blocks(rows):
    return jnp.concatenate(
        [rows[:, h * HEAD : (h + 1) * HEAD] for h in range(LOCAL_HEADS)], axis=0
    )


def store_pieces(out, j, total):
    for piece in range(RANK // 8):
        at = j * (RANK // 8) + piece
        out[at // NZ, at % NZ] = lane_blocks(total[piece * 8 : (piece + 1) * 8]).astype(BF16)


PIECES = (4, NZ, 40, 128)
LOWS = (2, CLIP, RANK)


def attend(steps, after, place, arrays, peer, ups, *lows):
    first, count = lows[0].dtype == F32, len(steps)
    shapes = [(PIECES, BF16)] * count + [(LOWS, F32)] * 2
    if first:
        shapes += [((2, 2 * CLIP, RANK), BF16), ((2, 8, RANK), F32)]
    scratch = [((count, 2, RANK, SHARD), BF16)] + [((count, 2 * CLIP, SHARD), BF16)] * 2
    kernel = functools.partial(attend_kernel, steps, first, len(after))
    given = [ups[step] for step in steps]
    return call(
        kernel, "attend", shapes, scratch, place, (*arrays, peer, *lows, *given), after
    )


def down_kernel(after, place, nown, peer, mine0, mine1, peer0, peer1, *refs):
    *outs, dlow, totals = refs[after:]
    for j in range(2):
        for clip in range(2):
            total = (mine0, mine1)[clip][j] + (peer1, peer0)[clip][j]
            dlow[j * RANK : (j + 1) * RANK, clip * CLIP : (clip + 1) * CLIP] = total.astype(BF16).T
    for shift in range(NY):
        shard = pl.multiple_of(lax.rem(place[1] + shift, NY) * SHARD, SHARD)
        normed = jnp.concatenate([nown[:, pl.ds(shard, SHARD)], peer[4, :, pl.ds(shard, SHARD)]], axis=0)
        totals[shift] = dot(dlow[...], normed, 1, 0)
        for step, out in enumerate(outs):
            first = lax.rem(place[3] + step, NX) * (2 * RANK // NX)
            for z in range(NZ):
                rows = totals[shift, pl.ds(pl.multiple_of(first + z * 8, 8), 8), :]
                out[shift, z] = lane_blocks(rows).astype(BF16)


def down_grads(place, nown, peer, dlows, *after):
    shapes = [((NY, *PIECES[1:]), BF16)] * NX
    scratch = [((2 * RANK, 2 * CLIP), BF16), ((NY, 2 * RANK, SHARD), F32)]
    kernel = functools.partial(down_kernel, len(after))
    return call(kernel, "down_grads", shapes, scratch, place, (nown, peer, *dlows), after)


def sum_y_kernel(place, *refs):
    parts, outs = refs[:4], refs[4:]
    x = place[3]
    for quarter in range(4):
        source = lax.rem(quarter + x, 4)
        for z in range(NZ):
            total = sum(r[source, z].astype(F32) for r in parts)
            outs[quarter][z] = total.astype(BF16)


def sum_y(place, parts):
    return pl.pallas_call(
        sum_y_kernel,
        out_shape=[jax.ShapeDtypeStruct(PIECES[1:], BF16)] * 4,
        in_specs=[pl.BlockSpec(memory_space=pltpu.SMEM)]
        + [pl.BlockSpec(memory_space=pltpu.VMEM)] * 4,
        out_specs=[pl.BlockSpec(memory_space=pltpu.VMEM)] * 4,
        compiler_params=pltpu.CompilerParams(vmem_limit_bytes=VMEM_LIMIT),
        cost_estimate=SMALL,
        name="sum_y",
    )(place, *parts)


def sum_x_kernel(*refs):
    parts, outs = refs[:4], refs[4:]
    for step in range(NY):
        outs[step][...] = sum(r[step].astype(F32) for r in parts).astype(BF16)


def sum_x(parts):
    return pl.pallas_call(
        sum_x_kernel,
        out_shape=[jax.ShapeDtypeStruct(PIECES[1:], BF16)] * NY,
        in_specs=[pl.BlockSpec(memory_space=pltpu.VMEM)] * 4,
        out_specs=[pl.BlockSpec(memory_space=pltpu.VMEM)] * NY,
        compiler_params=pltpu.CompilerParams(vmem_limit_bytes=VMEM_LIMIT),
        cost_estimate=SMALL,
        name="sum_x",
    )(*parts)


def join_kernel(*refs):
    ups, downs, out = refs[:4], refs[4:8], refs[8]
    for z in range(NZ):
        up = sum(r[z].astype(F32) for r in ups)
        down = sum(r[z].astype(F32) for r in downs)
        out[z] = jnp.concatenate([up, down], axis=0).astype(BF16)


def join(ups, downs):
    return pl.pallas_call(
        join_kernel,
        out_shape=jax.ShapeDtypeStruct((NZ, 80, 128), BF16),
        in_specs=[pl.BlockSpec(memory_space=pltpu.VMEM)] * 8,
        out_specs=pl.BlockSpec(memory_space=pltpu.VMEM),
        compiler_params=pltpu.CompilerParams(vmem_limit_bytes=VMEM_LIMIT),
        cost_estimate=SMALL,
        name="join",
    )(*ups, *downs)


def finish_kernel(factor, place, own, first, second, first_peer, second_peer, down, up, flat):
    core, x = place[2], place[3]

    def write(step, ref):
        quarter = lax.rem(x + step, 4)
        for z in range(NZ):
            part = ref[z].astype(F32) * factor
            for out, begin in ((up, 0), (flat, 40)):
                out[quarter * NZ + z] = jnp.concatenate(
                    [part[begin + h * 8 : begin + (h + 1) * 8] for h in range(LOCAL_HEADS)], axis=1
                )

    @pl.when(core == 0)
    def _():
        for step, ref in enumerate((own, second, first_peer, first)):
            write(step, ref)

    @pl.when(core == 1)
    def _():
        for step, ref in enumerate((second, second_peer, first, first_peer)):
            write(step, ref)

    for j in range(2):
        rows = flat[j * 2 * NZ : (j + 1) * 2 * NZ].reshape(RANK, SHARD)
        down[j] = rows.T


def finish(factor, place, *parts):
    return pl.pallas_call(
        functools.partial(finish_kernel, factor),
        out_shape=(
            jax.ShapeDtypeStruct((2, SHARD, RANK), F32),
            jax.ShapeDtypeStruct((4 * NZ, 8, SHARD), F32),
        ),
        in_specs=[pl.BlockSpec(memory_space=pltpu.SMEM)]
        + [pl.BlockSpec(memory_space=pltpu.VMEM)] * 5,
        out_specs=(pl.BlockSpec(memory_space=pltpu.VMEM),) * 2,
        scratch_shapes=[pltpu.VMEM((4 * NZ, 8, SHARD), F32)],
        compiler_params=pltpu.CompilerParams(vmem_limit_bytes=VMEM_LIMIT),
        name="finish",
    )(place, *parts)


def cross_x(part):
    other = send(part, lambda x, y, z, c: (x - 1, y, z, 1) if c == 0 else (x, y, z, 0))
    own = send(part, lambda x, y, z, c: (x, y, z, 0) if c == 0 else (x + 1, y, z, 1))
    return own, other


def local(states, steps, q, k, v, g, down_maps, up_maps):
    dp, fsdp = lax.axis_index("dp"), lax.axis_index("fsdp")
    core, x_lo, y = dp % 2, fsdp // NY, fsdp % NY
    x = (dp // (2 * NZ)) * 2 + x_lo
    place = jnp.stack([x_lo ^ core, y, core, x]).astype(jnp.int32)
    weight = (steps[0].astype(F32) + 1.0) / NSTEPS
    weight = jnp.full((8, RANK), weight, F32)

    down_part = lax.dynamic_index_in_dim(down_maps, core, 0, keepdims=False)
    up_part = lax.dynamic_index_in_dim(up_maps, core, 0, keepdims=False)
    nown, nsend = normalize(place, states, q, k, v, g)
    across, after, before = (send_y(down_part, -step) for step in (2, 1, 3))
    up = jnp.stack(cross_x(up_part))
    nsend, up, across, after, before = lax.optimization_barrier((nsend, up, across, after, before))
    downs = cross_x(jnp.stack([down_part, after, across, before]))
    ups = [up] + [send_y(up, -step) for step in range(1, NY)]
    peer = swap_cores(nsend)

    lows = lower(place, nown, peer, *downs, weight)
    lows = [*lows, *(swap_cores(part) for part in lows)]
    rows = (place, (q, k, v, g), peer, ups)
    gups = [None] * NY
    gups[1], gups[3], gups[0], *dlow, low, weights = attend((1, 3, 0), (), *rows, *lows)
    gups[1], gups[3] = send_y(gups[1], 1), send_y(gups[3], 3)
    gups[2], *dlow = attend((2,), (), *rows, low, weights, *dlow)
    gups[2] = send_y(gups[2], 2)
    dlows = [*dlow, *(swap_cores(part) for part in dlow)]
    gdowns = scatter_x(down_grads(place, nown, peer, dlows))
    ups = scatter_x(sum_y(place, gups))
    downs = scatter_y(sum_x(gdowns))
    eighths = join(ups, downs)
    eighths = exchange_z(eighths)
    piece = jnp.sum(eighths.astype(F32), axis=0).astype(BF16)
    quarter = exchange_z(jnp.broadcast_to(piece, (NZ, 80, 128)))

    first = send(
        quarter, lambda x, y, z, c: (x + 2, y, z, 1) if c == 0 else (x + 1, y, z, 0)
    )
    second = send(
        quarter, lambda x, y, z, c: (x, y, z, 1) if c == 0 else (x - 1, y, z, 0)
    )
    first_peer = swap_cores(first)
    second_peer = swap_cores(second)
    data_count = lax.axis_size("dp") * lax.axis_size("fsdp")
    factor = 1.0 / math.sqrt(CLIP * data_count)
    grad_down, grad_up = finish(
        factor, place, quarter, first, second, first_peer, second_peer
    )
    return (grad_down, grad_up.reshape(2, RANK, SHARD))


def solution(mesh):
    in_specs = (
        P(("dp", "fsdp"), None),
        P(("dp", "fsdp")),
        P(("dp", "fsdp"), None),
        P(("dp", "fsdp"), None),
        P(("dp", "fsdp"), None),
        P(("dp", "fsdp"), None),
        P(None, "fsdp", None),
        P(None, None, "fsdp"),
    )
    out_specs = (P(None, "fsdp", None), P(None, None, "fsdp"))
    return jax.shard_map(local, mesh=mesh, in_specs=in_specs, out_specs=out_specs, check_vma=False)
```
